32 devices in a mesh: pair: 2 (over y), grp: 4 (over z), seq: 4 (over x, core).
Axes of the slice: x: 2, y: 2, z: 4, core: 2. Of those that a mesh axis runs over, the one named last changes fastest.
Arguments:
- series: float32 [4, 8192, 64], P('grp', 'seq', 'pair'), may hold values from -8 to 8
- time_blocks: int32 [4, 4], P('grp'), may hold values from 0 to 31
- freq_blocks: int32 [4, 4], P('grp'), may hold values from 0 to 31
- positives: int32 [4], replicated, may hold values from 0 to 3, each once
- conv_weight: bfloat16 [2, 1024, 512], P('pair'), may hold values from -0.25 to 0.25
- proj_weight: bfloat16 [2, 1024, 128], P('pair'), may hold values from -0.1875 to 0.1875
Outputs:
- encoded: bfloat16 [2, 4, 4096, 1024], P('pair', 'grp', 'seq')
- loss_value: float32 [], replicated
- grad_conv: float32 [2, 1024, 512], P('pair', ('grp', 'seq'))
- grad_proj: float32 [2, 1024, 128], P('pair', 'grp')
The draws below stay inside these ranges and needn't reach their ends.
Inputs may be any that keep to these rules, and one draw needn't show every extreme that they name: `positives`: each of 0 to 3 stands once.
All inputs are finite; a program needn't handle non-finite values.
Results may differ from the reference program's by a relative error of at most 0.0042.
Values may be sent and summed in bfloat16 or wider, within the bound.
No kernel may reach another device: no remote copies, remote signals or barrier semaphores. Data moves between devices by JAX's collectives and lax.ppermute only.
A program may use at most 128 MiB of HBM per device.

```python
import math
import jax
import jax.numpy as jnp
from jax import lax

C = 64
H = 1024
E = 128
K = 8
SEQLEN = 8192
B = 4
MBLK = 256
NBLK = 32
NMASK = 4


def draw_series(key, part):
    key_noise, key_scale, key_common, key_taps, key_mix, key_sign = jax.random.split(jax.random.fold_in(key, 7), 6)
    scales = jnp.exp(jax.random.uniform(key_scale, (B, 1, C), jnp.float32, math.log(0.3), math.log(3.0)))
    mixing = jnp.exp(jax.random.uniform(key_mix, (B, 1, C), jnp.float32, math.log(1.0), math.log(3.0)))
    flips = jax.random.uniform(key_sign, (B, 1, C), jnp.float32, 0.0, 1.0)
    mixing = jnp.where(flips < 0.5, -mixing, mixing)
    taps = jax.random.normal(key_taps, (B, 8), jnp.float32) / math.sqrt(8.0)
    source = jax.random.normal(key_common, (B, SEQLEN), jnp.float32)
    common = taps[:, 0:1] * source
    for offset in range(1, 8):
        common = common + taps[:, offset:offset + 1] * jnp.roll(source, offset, axis=1)
    progress = jnp.arange(SEQLEN, dtype=jnp.float32) / SEQLEN
    envelope = jnp.exp(math.log(3.0) * (progress - 1.0))[None, :, None]
    fluctuation = jax.random.truncated_normal(key_noise, -4.0, 4.0, (B, SEQLEN, C), jnp.float32)
    values = (fluctuation * scales + mixing * common[:, :, None]) * envelope
    return jnp.clip(values, -8.0, 8.0)


def set_ends(entries, stream_key, low, largest):
    extent = entries.shape
    spot = [jax.random.randint(jax.random.fold_in(stream_key, axis), (), 0, extent[axis]) for axis in range(len(extent))]
    entries = entries.at[tuple(spot)].set(low)
    longest = extent.index(max(extent))
    spot[longest] = (spot[longest] + 1) % extent[longest]
    return entries.at[tuple(spot)].set(largest)


def block_scale(key, dims, shards, least, high):
    def one(axis_at, blocks):
        heights = jax.random.uniform(jax.random.fold_in(jax.random.fold_in(key, 6), axis_at), (blocks,), jnp.float32, least / len(shards), high / len(shards))
        return jnp.repeat(jnp.exp(heights), dims[axis_at] // blocks).reshape((-1,) + (1,) * (len(dims) - axis_at - 1))

    factor_of = one(*shards[0])
    for cut in shards[1:]:
        factor_of = factor_of * one(*cut)
    return factor_of


def centred(stream_key, extent, scale, bound, cuts=(), held_as=jnp.bfloat16):
    array = jax.random.normal(stream_key, extent, jnp.float32) * scale
    if len(cuts) > 0:
        array = block_scale(stream_key, extent, cuts, -0.22, 0.18) * array
    return jnp.clip(array, min=-bound, max=bound).astype(held_as)


def setup_inputs(seed: int = 0) -> dict:
    streams_of = jax.random.split(jax.random.key(seed), 7)
    series = draw_series(jax.random.fold_in(streams_of[6], 71), 0)
    time_blocks = set_ends(jax.random.randint(streams_of[1], (B, NMASK), 0, NBLK), jax.random.fold_in(streams_of[1], 1), 0, NBLK - 1).astype(jnp.int32)
    freq_blocks = set_ends(jax.random.randint(streams_of[2], (B, NMASK), 0, NBLK), jax.random.fold_in(streams_of[2], 1), 0, NBLK - 1).astype(jnp.int32)
    positives = jax.random.permutation(streams_of[3], B).astype(jnp.int32)
    conv_weight = centred(streams_of[4], (2, H, K * C), (K * C) ** -0.5, 0.25, ((0, 2),))
    proj_weight = centred(streams_of[5], (2, H, E), H ** -0.5, 0.1875, ((0, 2),))
    return {"series": series, "time_blocks": time_blocks, "freq_blocks": freq_blocks, "positives": positives, "conv_weight": conv_weight, "proj_weight": proj_weight}


TAU = 0.2
LOSS_SCALE = 256.0

def gelu_slope(values):
    output, pullback = jax.vjp(lambda argument: jax.nn.gelu(argument, approximate=True), values)
    return (output, pullback(jnp.ones_like(values))[0])

def embed(pooled, projection):
    latent = jnp.dot(pooled, projection, precision=lax.Precision.HIGHEST)
    return latent * lax.rsqrt(lax.optimization_barrier(jnp.sum(latent * latent, axis=1, keepdims=True)) + 1e-06)

def contrast(time_emb, freq_emb, positives):
    logits = jnp.dot(time_emb, freq_emb.T, precision=lax.Precision.HIGHEST) / TAU
    number = logits.shape[0]
    target = (positives[:, None] == jnp.arange(number, dtype=jnp.int32)[None, :]).astype(logits.dtype)
    exponent = jnp.exp(logits)
    row_lse = jnp.log(lax.optimization_barrier(jnp.sum(exponent, axis=1)))
    col_lse = jnp.log(lax.optimization_barrier(jnp.sum(exponent, axis=0)))
    picked = jnp.sum(target * logits)
    return (jnp.sum(row_lse) + jnp.sum(col_lse) - 2.0 * picked) / (2.0 * number)

def reference(series, time_blocks, freq_blocks, positives, conv_weight, proj_weight):
    position = jnp.arange(SEQLEN, dtype=jnp.int32) // MBLK

    def keep_mask(blocks):
        listed = jnp.any(blocks[:, :, None] == position[None, None, :], axis=1)
        return jnp.where(listed, 0.0, 1.0).astype(jnp.bfloat16)[:, :, None]
    time_in = series.astype(jnp.bfloat16) * keep_mask(time_blocks)
    spectrum = jnp.fft.fft(series, axis=1)
    real_part = jnp.real(spectrum)
    imag_part = jnp.imag(spectrum)
    energy = (real_part * real_part + imag_part * imag_part) / SEQLEN
    freq_in = jnp.sqrt(1.0 + energy).astype(jnp.bfloat16) * keep_mask(freq_blocks)
    half_rim = K // 2

    def patch_rows(signal):
        padded = jnp.pad(signal, ((half_rim, half_rim), (0, 0)))
        return jnp.concatenate([padded[offset:offset + SEQLEN] for offset in range(K)], axis=1)

    def encode(inputs, weight):

        def single(signal):
            patches = patch_rows(signal)
            preact = lax.dot_general(patches, weight, (((1,), (1,)), ((), ())), preferred_element_type=jnp.float32)
            active = jax.nn.gelu(preact, approximate=True)
            pairs = active.reshape(SEQLEN // 2, 2, H)
            halved = ((pairs[:, 0] + pairs[:, 1]) * 0.5).astype(jnp.bfloat16)
            return (halved, lax.optimization_barrier(jnp.mean(active, axis=0)))
        return lax.map(single, inputs)

    def conv_grad(inputs, weight, scaled):

        def accumulate(running, element):
            signal, factor = element
            patches = patch_rows(signal)
            preact = lax.dot_general(patches, weight, (((1,), (1,)), ((), ())), preferred_element_type=jnp.float32)
            _, slopes = gelu_slope(preact)
            upstream = (factor[None, :] * slopes).astype(jnp.bfloat16)
            update = lax.dot_general(upstream, patches, (((0,), (0,)), ((), ())), preferred_element_type=jnp.float32)
            return (running + update, None)
        result, _ = lax.scan(accumulate, jnp.zeros((H, K * C), jnp.float32), (inputs, scaled))
        return result
    enc_time, pool_time = encode(time_in, conv_weight[0])
    enc_freq, pool_freq = encode(freq_in, conv_weight[1])
    proj_time = proj_weight[0].astype(jnp.float32)
    proj_freq = proj_weight[1].astype(jnp.float32)
    emb_time, pull_time = jax.vjp(embed, pool_time, proj_time)
    emb_freq, pull_freq = jax.vjp(embed, pool_freq, proj_freq)
    loss_value, emb_grads = jax.value_and_grad(contrast, argnums=(0, 1))(emb_time, emb_freq, positives)
    dpool_time, dproj_time = pull_time(emb_grads[0] * LOSS_SCALE)
    dpool_freq, dproj_freq = pull_freq(emb_grads[1] * LOSS_SCALE)
    grad_time = conv_grad(time_in, conv_weight[0], dpool_time / SEQLEN)
    grad_freq = conv_grad(freq_in, conv_weight[1], dpool_freq / SEQLEN)
    encoded = jnp.stack([enc_time, enc_freq])
    grad_conv = jnp.stack([grad_time, grad_freq])
    grad_proj = jnp.stack([dproj_time, dproj_freq])
    return (encoded, loss_value, grad_conv, grad_proj)
```

```python
import functools
import math

import jax
import jax.numpy as jnp
import ml_dtypes
import numpy as np
from jax import lax
from jax.experimental import pallas as pl
from jax.experimental.pallas import tpu as pltpu
from jax.sharding import PartitionSpec as P

TAU = 0.2
LOSS_SCALE = 256.0
LANES = 128
ROOT = math.sqrt(2.0 / math.pi)
CUBIC = 0.044715
F32 = jnp.float32
BF16 = jnp.bfloat16

VMEM = pl.BlockSpec(memory_space=pltpu.VMEM)
SMEM = pl.BlockSpec(memory_space=pltpu.SMEM)


def call(kernel, out_shape, in_specs, scratch=(), flops=0, moved=0, **kwargs):
    single = not isinstance(out_shape, (list, tuple))
    return pl.pallas_call(
        kernel,
        out_shape=out_shape,
        in_specs=in_specs,
        out_specs=VMEM if single else [VMEM] * len(out_shape),
        scratch_shapes=list(scratch),
        compiler_params=pltpu.CompilerParams(vmem_limit_bytes=56 * 1024 * 1024),
        cost_estimate=pl.CostEstimate(flops=flops, bytes_accessed=moved, transcendentals=0),
        **kwargs,
    )


def split_high_low(table):
    high = table.astype(ml_dtypes.bfloat16)
    low = (table - high.astype(np.float64)).astype(ml_dtypes.bfloat16)
    return high, low


def fourier_tables(full_len):
    first_count = 2 * LANES
    rest = full_len // first_count
    top = np.arange(first_count)
    first = (2 * np.arange(LANES)[None, :] + np.arange(2)[:, None]).reshape(-1)
    low = np.arange(rest)
    angle = (top[:, None] * first[None, :] % first_count) * (2.0 * np.pi / first_count)
    high, small = split_high_low(np.concatenate([np.cos(angle), -np.sin(angle)], axis=1))
    stage_one = np.concatenate([high, small, high], axis=0)
    turn = (low[:, None] * first[None, :] % full_len) * (2.0 * np.pi / full_len)
    angle = (low[:, None] * low[None, :] % rest) * (2.0 * np.pi / rest)
    cos, sin = np.cos(angle), np.sin(angle)
    high, small = split_high_low(np.block([[cos, sin], [-sin, cos]]))
    stage_two = np.concatenate([high, small, high], axis=1)
    return stage_one, np.cos(turn).astype(np.float32), np.sin(turn).astype(np.float32), stage_two


def arrange_kernel(groups, rest, scalars, series, *outs):
    *pieces, held = outs
    me = scalars[0]
    length, chans = series.shape
    tops = length // rest
    stacked = LANES // tops
    lows = rest // stacked
    for low in range(lows):
        rows = [series[pl.ds(part * lows + low, tops, stride=rest), :] for part in range(stacked)]
        held[pl.ds(low, chans, stride=lows), :] = jnp.concatenate(rows, axis=0).T
    size = chans // groups * lows
    for turn in range(groups):
        start = pl.multiple_of((me ^ turn) * size, 8)
        pieces[turn][...] = held[pl.ds(start, size), :]


def time_kernel(series, out):
    length, chans = series.shape
    for block in range(length // (2 * LANES)):
        for parity in range(2):
            rows = series[pl.ds(2 * LANES * block + parity, LANES, stride=2), :]
            out[chans * parity : chans * (parity + 1), LANES * block : LANES * (block + 1)] = rows.T.astype(BF16)


def high_low(values):
    high = values.astype(BF16)
    return high, (values - high.astype(F32)).astype(BF16)


def fourier_kernel(groups, full_len, scalars, time_view, stage_one, turn_cos, turn_sin, stage_two, *refs):
    pieces = refs[:groups]
    own, pay, gathered, mags, wire = refs[groups:]
    me, branch = scalars[0], scalars[1]
    rest = full_len // (2 * LANES)
    tops = 2 * LANES // groups
    stacked = LANES // tops
    lows = rest // stacked
    rows = pieces[0].shape[0]
    chans = rows // lows
    for turn in range(groups):
        gathered[turn] = pieces[turn][...]
    blocks = [gathered[source ^ me] for source in range(groups)]
    parts = [
        jnp.concatenate([block[:, part * tops : (part + 1) * tops] for block in blocks], axis=1)
        for part in range(stacked)
    ]
    steps = jnp.concatenate(parts, axis=0)
    high, low = high_low(steps)
    first = jnp.dot(jnp.concatenate([high, high, low], axis=1), stage_one[...], preferred_element_type=F32)
    first = first.reshape(stacked, chans, lows, 4 * LANES)
    cos = turn_cos[...].reshape(stacked, 1, lows, 2 * LANES)
    sin = turn_sin[...].reshape(stacked, 1, lows, 2 * LANES)
    part_re, part_im = first[..., : 2 * LANES], first[..., 2 * LANES :]
    turned_re = part_re * cos + part_im * sin
    turned_im = part_im * cos - part_re * sin
    columns = [
        jnp.concatenate(
            [turned_re[part, chan] for part in range(stacked)]
            + [turned_im[part, chan] for part in range(stacked)],
            axis=0,
        )
        for chan in range(chans)
    ]
    high, low = high_low(jnp.concatenate(columns, axis=1))
    second = jnp.dot(stage_two[...], jnp.concatenate([high, high, low], axis=0), preferred_element_type=F32)
    spec_re, spec_im = second[:rest], second[rest:]
    magnitude = jnp.sqrt(1.0 + (spec_re * spec_re + spec_im * spec_im) * (1.0 / full_len))
    for chan in range(chans):
        for parity in range(2):
            at = (parity * chans + chan) * rest
            mags[at : at + rest, :] = magnitude[:, (2 * chan + parity) * LANES : (2 * chan + parity + 1) * LANES]
    per_chunk = rest // groups
    for block in range(rest):
        chunk, inner = block // per_chunk, block % per_chunk
        wire[2 * chans * chunk : 2 * chans * (chunk + 1), LANES * inner : LANES * (inner + 1)] = mags[
            pl.ds(block, 2 * chans, stride=rest), :
        ]

    @pl.when(branch == 0)
    def _():
        own[...] = time_view[...]
        pay[...] = wire[...].astype(BF16)

    @pl.when(branch != 0)
    def _():
        own[...] = wire[...].astype(BF16)
        pay[...] = time_view[...]


def gelu_parts(values):
    square = values * values
    curve = jnp.tanh(values * (ROOT + (ROOT * CUBIC) * square))
    half = 0.5 * values
    return square, curve, half


def stack_rows(window, count):
    return jnp.concatenate([window[6 + shift : 6 + shift + count] for shift in range(4)], axis=1).astype(BF16)


def odd_rows(even, following):
    lane = lax.broadcasted_iota(jnp.int32, even.shape, 1)
    return jnp.where(lane < LANES // 2, pltpu.roll(even, LANES // 2, 1), pltpu.roll(following, LANES // 2, 1))


def slope_kernel(groups, tile, scalars, time_blocks, freq_blocks, weight, projection, *refs):
    count = 2 * groups
    slots = refs[:count]
    grads = refs[count:-7]
    payload, near, flat, tall, odd, total, pool = refs[-7:]
    me, branch = scalars[0], scalars[1]
    grp_pos = scalars[2]
    half_rows, chunk = slots[0].shape
    own_chan = half_rows // 2
    chans = own_chan // groups
    aligned = chans % 8 == 0
    halves = chunk * groups
    flat[:, :LANES] = jnp.zeros((LANES, LANES), F32)
    flat[:, LANES + halves :] = jnp.zeros((LANES, LANES), F32)
    tall[:8, :] = jnp.zeros((8, LANES), F32)
    tall[8 + halves :, :] = jnp.zeros((16, LANES), F32)
    for flip in range(2):
        for turn in range(groups):
            slot = slots[flip * groups + turn]
            side = branch ^ flip
            source = me ^ turn

            by_steps = branch == 0 if aligned else branch >= 0

            @pl.when(by_steps)
            def _(slot=slot, side=side, source=source):
                for parity in range(2):
                    row = pl.multiple_of(parity * 2 * own_chan + side * own_chan, 8)
                    lane = pl.multiple_of(LANES + source * chunk, LANES)
                    flat[pl.ds(row, own_chan), pl.ds(lane, chunk)] = slot[
                        parity * own_chan : (parity + 1) * own_chan, :
                    ].astype(F32)

            if not aligned:
                continue

            @pl.when(branch != 0)
            def _(slot=slot, side=side, source=source):
                for part in range(groups):
                    values = slot[2 * chans * part : 2 * chans * (part + 1), :].astype(F32)
                    for parity in range(2):
                        row = pl.multiple_of(parity * 2 * own_chan + side * own_chan + source * chans, chans)
                        flat[pl.ds(row, chans), LANES + part * chunk : LANES + (part + 1) * chunk] = values[
                            parity * chans : (parity + 1) * chans
                        ]

    def mask(block, _):
        keep = jnp.float32(1.0)
        for entry in range(time_blocks.shape[1]):
            listed = jnp.where(branch == 0, time_blocks[0, entry], freq_blocks[0, entry])
            keep = jnp.where(listed == block, 0.0, keep)
        at = pl.multiple_of(LANES + block * LANES, LANES)
        values = flat[:, pl.ds(at, LANES)] * keep
        flat[:, pl.ds(at, LANES)] = values
        tall[pl.ds(pl.multiple_of(8 + block * LANES, 8), LANES), :] = values.T
        return 0

    lax.fori_loop(0, halves // LANES, mask, 0)
    begin = pl.multiple_of(me * chunk, LANES)
    near[...] = tall[pl.ds(begin, chunk + 24), :]

    def shift(block, _):
        at = pl.multiple_of(block * tile, tile)
        window = tall[pl.ds(at, tile + 8), :]
        odd[pl.ds(at, tile), :] = odd_rows(window[:tile], window[1 : tile + 1])
        return 0

    lax.fori_loop(0, halves // tile, shift, 0)
    tail = tall[halves : halves + 24, :]
    odd[halves:, :] = odd_rows(tail[:16], tail[1:17])
    total[...] = jnp.zeros_like(total)
    pool[...] = jnp.zeros_like(pool)

    def step(index, _):
        at = pl.multiple_of(index * tile, tile)
        window = flat[:, pl.ds(at, tile + 2 * LANES)]
        shifted = jnp.concatenate(
            [window[:, LANES + move : LANES + move + tile] for move in range(-2, 3)], axis=0
        ).astype(BF16)
        sums = pool[...]
        for parity in range(2):
            columns = shifted[LANES // 2 * parity : LANES // 2 * parity + 4 * LANES]
            preact = jnp.dot(weight[...], columns, preferred_element_type=F32)
            square, curve, half = gelu_parts(preact)
            active = half + half * curve
            for part in range(tile // LANES):
                sums = sums + active[:, part * LANES : (part + 1) * LANES]
            slope = (0.5 + 0.5 * curve) + (half * (1.0 - curve * curve)) * (ROOT + (3.0 * ROOT * CUBIC) * square)
            source = tall if parity == 0 else odd
            rows = stack_rows(source[pl.ds(at, tile + 16), :], tile)
            total[...] += jnp.dot(slope.astype(BF16), rows, preferred_element_type=F32)
        pool[...] = sums
        return 0

    lax.fori_loop(0, halves // tile, step, 0)
    share = len(grads)
    rows = weight.shape[0] // share
    column = jnp.sum(pool[...], axis=1, keepdims=True)
    latent = jnp.sum(column * projection[...].astype(F32), axis=0, keepdims=True)
    line = jnp.broadcast_to(column, (column.shape[0], LANES)).T[0:1, :]
    payload[...] = jnp.zeros_like(payload)
    total_devices = payload.shape[0]
    for device in range(total_devices):
        target = device // groups % share
        payload[device, 0:1, :] = latent
        payload[device, 1:2, 0:rows] = line[:, target * rows : (target + 1) * rows]
    for turn in range(share):
        start = pl.multiple_of((grp_pos ^ turn) * rows, 8)
        grads[turn][...] = total[pl.ds(start, rows), :]


def encode_kernel(near, weight, out):
    tile = out.shape[0]
    at = pl.multiple_of(pl.program_id(0) * tile, tile)
    window = near[pl.ds(at, tile + 24), :]
    even = window[: tile + 16]
    shifted = odd_rows(even, window[1 : tile + 17])
    sums = None
    for rows in (even, shifted):
        preact = lax.dot_general(
            stack_rows(rows, tile), weight[...], (((1,), (1,)), ((), ())), preferred_element_type=F32
        )
        _, curve, half = gelu_parts(preact)
        active = half + half * curve
        sums = active if sums is None else sums + active
    out[...] = (sums * 0.5).astype(BF16)


def loss_kernel(groups, share, full_len, scalars, positives, arrived, projection, loss, factors, grad):
    branch, grp_pos = scalars[1], scalars[2]
    batch = positives.shape[0]
    exact = lax.Precision.HIGHEST
    latents = []
    for side in range(2):
        lines = []
        for item in range(batch):
            base = (side * share + item) * groups
            line = arrived[base, 0:1, :]
            for turn in range(1, groups):
                line = line + arrived[base + turn, 0:1, :]
            lines.append(line * (1.0 / full_len))
        latents.append(jnp.concatenate(lines, axis=0))
    scale = [lax.rsqrt(jnp.sum(latent * latent, axis=1, keepdims=True) + 1e-06) for latent in latents]
    embs = [latent * factor for latent, factor in zip(latents, scale)]
    logits = lax.dot_general(embs[0], embs[1], (((1,), (1,)), ((), ())), precision=exact, preferred_element_type=F32) / TAU
    row = lax.broadcasted_iota(jnp.int32, logits.shape, 0)
    col = lax.broadcasted_iota(jnp.int32, logits.shape, 1)
    target = jnp.zeros_like(logits)
    for item in range(batch):
        target = jnp.where((row == item) & (col == positives[item]), 1.0, target)
    power = jnp.exp(logits)
    row_sum = jnp.sum(power, axis=1, keepdims=True)
    col_sum = jnp.sum(power, axis=0, keepdims=True)
    value = (
        jnp.sum(jnp.log(row_sum), axis=(0, 1), keepdims=True)
        + jnp.sum(jnp.log(col_sum), axis=(0, 1), keepdims=True)
        - 2.0 * jnp.sum(target * logits, axis=(0, 1), keepdims=True)
    ) / (2.0 * batch)
    loss[...] = jnp.broadcast_to(value, loss.shape)
    slope = (power / row_sum + power / col_sum - 2.0 * target) * (LOSS_SCALE / (2.0 * batch * TAU))
    emb_grads = [
        lax.dot_general(slope, embs[1], (((1,), (0,)), ((), ())), precision=exact, preferred_element_type=F32),
        lax.dot_general(slope.T, embs[0], (((1,), (0,)), ((), ())), precision=exact, preferred_element_type=F32),
    ]
    own = []
    for side in range(2):
        inner = jnp.sum(emb_grads[side] * embs[side], axis=1, keepdims=True)
        own.append(scale[side] * (emb_grads[side] - embs[side] * inner))
    latent_grad = jnp.where(branch == 0, own[0], own[1])
    rows = projection.shape[0]
    weights = projection[...].astype(F32)
    lane = lax.broadcasted_iota(jnp.int32, (rows, LANES), 1)
    spread = jnp.zeros((rows, LANES), F32)
    for item in range(batch):
        column = jnp.sum(weights * latent_grad[item : item + 1, :], axis=1, keepdims=True) * (1.0 / full_len)
        spread = jnp.where(lane == item, column, spread)
    factors[...] = spread
    for turn in range(groups):
        lines = [arrived[(branch * share + item) * groups + turn, 1:2, :] for item in range(batch)]
        lines = lines + [jnp.zeros((8 - batch % 8, LANES), F32)] if batch % 8 else lines
        sums = jnp.concatenate(lines, axis=0).T * (1.0 / full_len)
        value = sums[:, 0:1] * latent_grad[0:1, :]
        for item in range(1, batch):
            value = value + sums[:, item : item + 1] * latent_grad[item : item + 1, :]
        grad[turn * rows : (turn + 1) * rows, :] = value[:rows]


def combine_kernel(share, scalars, factors, *refs):
    pieces, out = refs[:share], refs[share]
    grp_pos = scalars[2]
    values = factors[...]
    lane = lax.broadcasted_iota(jnp.int32, values.shape, 1)
    result = None
    for turn in range(share):
        column = jnp.sum(jnp.where(lane == (grp_pos ^ turn), values, 0.0), axis=1, keepdims=True)
        term = column * pieces[turn][...]
        result = term if result is None else result + term
    out[...] = result


def by_steps(slots, groups, seq_pos, branch):
    order = jnp.arange(groups, dtype=jnp.int32) ^ seq_pos
    result = []
    for flip in range(2):
        held = jnp.stack(slots[flip * groups : (flip + 1) * groups])
        rows, chunk = held.shape[1:]
        split = held[order].reshape(groups, groups, 2, rows // (2 * groups), chunk)
        moved = jnp.transpose(split, (1, 2, 0, 3, 4)).reshape(groups, rows, chunk)
        picked = jnp.where(branch == 0, held, moved[order])
        result += [picked[turn] for turn in range(groups)]
    return result


def body(series, time_blocks, freq_blocks, positives, conv_weight, proj_weight):
    groups = lax.axis_size("seq")
    share = lax.axis_size("grp")
    sides = lax.axis_size("pair")
    seq_pos = lax.axis_index("seq")
    branch = lax.axis_index("pair")
    grp_pos = lax.axis_index("grp")
    samples, length, own_chan = series.shape
    assert samples == 1 and sides == 2
    full_len = length * groups
    hidden, width = conv_weight.shape[1:]
    emb_dim = proj_weight.shape[2]
    rest = full_len // (2 * LANES)
    tops = 2 * LANES // groups
    lows = rest // (LANES // tops)
    chans = own_chan // groups
    scalars = jnp.stack([seq_pos, branch, grp_pos]).astype(jnp.int32)

    piece = jax.ShapeDtypeStruct((chans * lows, LANES), F32)
    with jax.named_scope("arrange"):
        pieces = call(
            functools.partial(arrange_kernel, groups, rest),
            [piece] * groups,
            [SMEM, VMEM],
            [pltpu.VMEM((own_chan * lows, LANES), F32)],
            flops=10**8,
            moved=2 * 10**6,
        )(scalars, series[0])
    pieces = [pieces[0]] + [
        lax.ppermute(pieces[turn], "seq", [(i, i ^ turn) for i in range(groups)]) for turn in range(1, groups)
    ]
    wire = jax.ShapeDtypeStruct((2 * own_chan, length // 2), BF16)
    with jax.named_scope("time_view"):
        time_view = call(time_kernel, wire, [VMEM], flops=10**8, moved=2 * 10**6)(series[0])
    tables = [jnp.asarray(table) for table in fourier_tables(full_len)]
    with jax.named_scope("fourier"):
        own, pay = call(
            functools.partial(fourier_kernel, groups, full_len),
            [wire, wire],
            [SMEM] + [VMEM] * (5 + groups),
            [
                pltpu.VMEM((groups, chans * lows, LANES), F32),
                pltpu.VMEM((2 * chans * rest, LANES), F32),
                pltpu.VMEM((2 * own_chan, length // 2), F32),
            ],
            flops=10**9,
            moved=4 * 10**6,
        )(scalars, time_view, *tables, *pieces)

    slots = [None] * (2 * groups)
    for flip in range(2):
        for turn in range(0, groups, 2):
            block = pay if flip else own
            if flip or turn:
                pairs = [
                    (p * groups + i, (p ^ flip) * groups + (i ^ turn)) for p in range(2) for i in range(groups)
                ]
                block = lax.ppermute(block, ("pair", "seq"), pairs)
            slots[flip * groups + turn] = block
    for flip in range(2):
        for turn in range(0, groups, 2):
            slots[flip * groups + turn + 1] = lax.ppermute(
                slots[flip * groups + turn], "seq", [(i, i ^ 1) for i in range(groups)]
            )

    if chans % 8:
        slots = by_steps(slots, groups, seq_pos, branch)

    rows = hidden // (share * groups)
    picked = lax.dynamic_index_in_dim(
        conv_weight[0].reshape(share, groups, rows, width), seq_pos, 1, keepdims=False
    ).reshape(share * rows, width)
    proj_groups = proj_weight[0].reshape(share, groups, rows, emb_dim)
    proj_picked = lax.dynamic_index_in_dim(proj_groups, seq_pos, 1, keepdims=False)
    proj_own = lax.dynamic_index_in_dim(proj_picked, grp_pos, 0, keepdims=False)
    proj_picked = proj_picked.reshape(share * rows, emb_dim)
    halves = full_len // 2
    near_len = length // 2
    devices = sides * share * groups
    tile = 512
    with jax.named_scope("slope"):
        *grads, payload, near = call(
            functools.partial(slope_kernel, groups, tile),
            [jax.ShapeDtypeStruct((rows, width), F32)] * share
            + [
                jax.ShapeDtypeStruct((devices, 8, LANES), F32),
                jax.ShapeDtypeStruct((near_len + 24, LANES), F32),
            ],
            [SMEM] * 3 + [VMEM] * (2 + 2 * groups),
            [
                pltpu.VMEM((LANES, halves + 2 * LANES), F32),
                pltpu.VMEM((halves + 24, LANES), F32),
                pltpu.VMEM((halves + 16, LANES), F32),
                pltpu.VMEM((share * rows, width), F32),
                pltpu.VMEM((share * rows, LANES), F32),
            ],
            flops=4 * halves * 2 * share * rows * width,
            moved=4 * 10**6,
        )(scalars, time_blocks, freq_blocks, picked, proj_picked, *slots)
    arrived = lax.all_to_all(payload, ("pair", "grp", "seq"), split_axis=0, concat_axis=0, tiled=True)
    grads = [grads[0]] + [
        lax.ppermute(grads[turn], "grp", [(i, i ^ turn) for i in range(share)]) for turn in range(1, share)
    ]
    enc_tile = 256
    with jax.named_scope("encode"):
        encoded = pl.pallas_call(
            encode_kernel,
            out_shape=jax.ShapeDtypeStruct((near_len, hidden), BF16),
            grid=(near_len // enc_tile,),
            in_specs=[VMEM, VMEM],
            out_specs=pl.BlockSpec((enc_tile, hidden), lambda i: (i, 0)),
            compiler_params=pltpu.CompilerParams(vmem_limit_bytes=56 * 1024 * 1024),
            cost_estimate=pl.CostEstimate(
                flops=2 * length * hidden * width, bytes_accessed=4 * 10**6, transcendentals=length * hidden
            ),
        )(near, conv_weight[0])
    with jax.named_scope("loss"):
        loss, factors, proj_share = call(
            functools.partial(loss_kernel, groups, share, full_len),
            [
                jax.ShapeDtypeStruct((8, LANES), F32),
                jax.ShapeDtypeStruct((rows, LANES), F32),
                jax.ShapeDtypeStruct((groups * rows, emb_dim), F32),
            ],
            [SMEM] * 2 + [VMEM] * 2,
            flops=10**7,
            moved=10**6,
        )(scalars, positives, arrived, proj_own)
    with jax.named_scope("combine"):
        conv_share = call(
            functools.partial(combine_kernel, share),
            jax.ShapeDtypeStruct((rows, width), F32),
            [SMEM] + [VMEM] * (1 + share),
            flops=10**6,
            moved=5 * 10**5,
        )(scalars, factors, *grads)
    return (encoded[None, None], loss[0, 0], conv_share[None], proj_share[None])


def solution(mesh):
    in_specs = (
        P("grp", "seq", "pair"),
        P("grp", None),
        P("grp", None),
        P(),
        P("pair", None, None),
        P("pair", None, None),
    )
    out_specs = (
        P("pair", "grp", "seq", None),
        P(),
        P("pair", ("grp", "seq"), None),
        P("pair", "grp", None),
    )
    return jax.shard_map(body, mesh=mesh, in_specs=in_specs, out_specs=out_specs, check_vma=False)
```

```python
import functools
import math

import jax
import jax.numpy as jnp
import ml_dtypes
import numpy as np
from jax import lax
from jax.experimental import pallas as pl
from jax.experimental.pallas import tpu as pltpu
from jax.sharding import PartitionSpec as P

TAU = 0.2
LOSS_SCALE = 256.0
LANES = 128
ROOT = math.sqrt(2.0 / math.pi)
CUBIC = 0.044715
F32 = jnp.float32
BF16 = jnp.bfloat16

VMEM = pl.BlockSpec(memory_space=pltpu.VMEM)
SMEM = pl.BlockSpec(memory_space=pltpu.SMEM)


def call(kernel, out_shape, in_specs, scratch=(), flops=0, moved=0, room=16, out_specs=None):
    single = not isinstance(out_shape, (list, tuple))
    return pl.pallas_call(
        kernel,
        out_shape=out_shape,
        in_specs=in_specs,
        out_specs=out_specs or (VMEM if single else [VMEM] * len(out_shape)),
        scratch_shapes=list(scratch),
        compiler_params=pltpu.CompilerParams(vmem_limit_bytes=room * 1024 * 1024),
        cost_estimate=pl.CostEstimate(flops=flops, bytes_accessed=moved, transcendentals=0),
    )


def split_high_low(table):
    high = table.astype(ml_dtypes.bfloat16)
    low = (table - high.astype(np.float64)).astype(ml_dtypes.bfloat16)
    return high, low


def lane_order(low_count):
    inner = min(low_count, LANES)
    parts = LANES // inner
    lane = np.arange(LANES)
    return parts * (lane % inner) + lane // inner


def fourier_tables(full_len):
    low_count = full_len // LANES
    first = np.arange(low_count)
    rest = np.arange(LANES)
    second = lane_order(low_count)
    angle = (first[:, None] * first[None, :] % low_count) * (2.0 * np.pi / low_count)
    high, small = split_high_low(np.concatenate([np.cos(angle), -np.sin(angle)], axis=0))
    stage_one = np.concatenate([high, small, high], axis=1)
    turn = (first[:, None] * rest[None, :] % full_len) * (2.0 * np.pi / full_len)
    angle = (rest[:, None] * second[None, :] % LANES) * (2.0 * np.pi / LANES)
    cos, sin = np.cos(angle), np.sin(angle)
    high, small = split_high_low(np.block([[cos, -sin], [sin, cos]]))
    stage_two = np.concatenate([high, small, high], axis=0)
    return stage_one, np.cos(turn).astype(np.float32), np.sin(turn).astype(np.float32), stage_two


def arrange_kernel(scalars, series, *pieces):
    me = scalars[0]
    for turn, piece in enumerate(pieces):
        piece[...] = series[me ^ turn]


def high_low(values):
    high = values.astype(BF16)
    return high, (values - high.astype(F32)).astype(BF16)


def keep_lanes(scalars, first, number, low_count, block_len):
    lane = lax.broadcasted_iota(jnp.int32, (8, LANES), 1)
    inner = min(low_count, LANES)
    parts = LANES // inner
    high = parts * (lane % inner) + lane // inner
    block = high * low_count // block_len
    keep = jnp.ones((8, LANES), F32)
    for entry in range(first, first + number):
        keep = jnp.where(block == scalars[entry], 0.0, keep)
    return keep[0:1]


def fourier_kernel(
    groups, full_len, block_len, listed, scalars, stage_one, turn_cos, turn_sin, stage_two, *refs
):
    pieces = refs[:groups]
    own, pay, gathered, steps, mags, views, wire = refs[groups:]
    me, branch = scalars[0], scalars[1]
    low_count = full_len // LANES
    chans, length = pieces[0].shape
    tops = length // LANES
    for turn in range(groups):
        gathered[turn] = pieces[turn][...]
    for source in range(groups):
        block = gathered[source ^ me]
        for top in range(tops):
            at = (source * tops + top) * chans
            steps[at : at + chans, :] = block[:, top * LANES : (top + 1) * LANES]
    columns = [steps[pl.ds(chan, low_count, stride=chans), :] for chan in range(chans)]
    high, low = high_low(jnp.concatenate(columns, axis=1))
    first = jnp.dot(stage_one[...], jnp.concatenate([high, high, low], axis=0), preferred_element_type=F32)
    cos, sin = turn_cos[...], turn_sin[...]
    turned = []
    for chan in range(chans):
        part = first[:, chan * LANES : (chan + 1) * LANES]
        part_re, part_im = part[:low_count], part[low_count:]
        turned.append(jnp.concatenate([part_re * cos + part_im * sin, part_im * cos - part_re * sin], axis=1))
    high, low = high_low(jnp.concatenate(turned, axis=0))
    second = jnp.dot(jnp.concatenate([high, high, low], axis=1), stage_two[...], preferred_element_type=F32)
    spec_re, spec_im = second[:, :LANES], second[:, LANES:]
    magnitude = jnp.sqrt(1.0 + (spec_re * spec_re + spec_im * spec_im) * (1.0 / full_len))
    mags[...] = magnitude.astype(BF16).astype(F32) * keep_lanes(scalars, 3 + listed, listed, low_count, block_len)
    time_keep = keep_lanes(scalars, 3, listed, low_count, block_len)
    for chan in range(chans):
        if low_count < LANES:
            turned_steps = columns[chan].T
            view = jnp.concatenate(
                [turned_steps[part * low_count : (part + 1) * low_count] for part in range(LANES // low_count)], axis=1
            )
        else:
            parts = low_count // LANES
            view = jnp.concatenate(
                [steps[pl.ds(chan + chans * part, LANES, stride=chans * parts), :].T for part in range(parts)], axis=0
            )
        views[chan * low_count : (chan + 1) * low_count, :] = view * time_keep

    def spread(held, out):
        for low in range(low_count):
            wire[chans * low : chans * (low + 1), :] = held[pl.ds(low, chans, stride=low_count), :]
        out[...] = wire[...].astype(BF16)

    @pl.when(branch == 0)
    def _():
        spread(views, own)
        spread(mags, pay)

    @pl.when(branch != 0)
    def _():
        spread(mags, own)
        spread(views, pay)


def gelu_parts(values):
    square = values * values
    curve = jnp.tanh(values * (ROOT + (ROOT * CUBIC) * square))
    half = 0.5 * values
    return square, curve, half


def stack_rows(window, count):
    return jnp.concatenate([window[6 + shift : 6 + shift + count] for shift in range(4)], axis=1).astype(BF16)


def shift_high(tile, low_count, step):
    inner = min(low_count, LANES)
    lane = lax.broadcasted_iota(jnp.int32, tile.shape, 1)
    if step < 0:
        moved = jnp.where(lane < inner, pltpu.roll(tile, (inner + 1) % LANES, 1), pltpu.roll(tile, inner % LANES, 1))
        return jnp.where(lane == 0, 0.0, moved)
    back = LANES - inner
    moved = jnp.where(lane < back, pltpu.roll(tile, back, 1), pltpu.roll(tile, (back - 1) % LANES, 1))
    return jnp.where(lane == LANES - 1, 0.0, moved)


def swap_units(values, outer, inner):
    unit = outer * inner * 8
    blocks = []
    for start in range(0, values.shape[0], unit):
        for second in range(inner):
            for first in range(outer):
                at = start + (first * inner + second) * 8
                blocks.append(values[at : at + 8])
    return jnp.concatenate(blocks, axis=0)


def prepare_kernel(groups, share, ready, scalars, weight, picked, stage_one, turn_cos, turn_sin, stage_two, *outs):
    full, part, *tables = outs
    me = scalars[0]
    full[...] = swap_units(weight[...].astype(F32).T, 2, 8).astype(BF16)
    if ready:
        rows = picked[...]
    else:
        size = weight.shape[0] // (share * groups)
        starts = [pl.multiple_of((group * groups + me) * size, 16) for group in range(share)]
        rows = jnp.concatenate([weight[pl.ds(start, size), :] for start in starts], axis=0)
    part[...] = swap_units(rows.astype(F32).T, 2, 8).astype(BF16)
    for table, out in zip((stage_one, turn_cos, turn_sin, stage_two), tables):
        out[...] = table[...]


def slope_kernel(groups, ready, merged, scalars, weights, projection, *refs):
    count = 1 if ready else 2 * groups
    slots = refs[:count]
    grads = refs[count:-6]
    payload, flat, odd, total, pool, split = refs[-6:]
    me, branch, grp_pos = scalars[0], scalars[1], scalars[2]
    lows = flat.shape[0] - 4
    low_count = 2 * lows
    share = len(grads)
    wide = 4 * LANES
    rows = grads[0].shape[0]
    if ready:
        flat[2 : 2 + lows] = slots[0][...].reshape(lows, LANES, LANES)
        heads = projection[...]
    else:
        for flip in range(2):
            for turn in range(groups):
                at = pl.multiple_of(((branch ^ flip) * groups + (me ^ turn)) * 16, 16)
                flat[2 : 2 + lows, pl.ds(at, 16), :] = slots[flip * groups + turn][...].reshape(lows, 16, LANES)
        starts = [pl.multiple_of((group * groups + me) * rows, 16) for group in range(share)]
        heads = jnp.concatenate([projection[pl.ds(start, rows), :] for start in starts], axis=0)
    for edge in range(2):
        flat[edge] = shift_high(flat[lows + edge].astype(F32), low_count, -1).astype(BF16)
        flat[lows + 2 + edge] = shift_high(flat[2 + edge].astype(F32), low_count, 1).astype(BF16)
    current = flat[0].astype(F32).reshape(8, 2, 8, LANES)
    for index in range(lows + 3):
        following = flat[index + 1].astype(F32).reshape(8, 2, 8, LANES)
        mixed = jnp.concatenate([current[:, 1:2], following[:, 0:1]], axis=1)
        odd[index] = mixed.reshape(LANES, LANES).astype(BF16)
        current = following
    total[...] = jnp.zeros_like(total)
    pool[...] = jnp.zeros_like(pool)

    def step(index, _):
        first = index * merged
        sums = pool[...]
        for source in (flat, odd):
            across = jnp.concatenate(
                [
                    jnp.concatenate([source[first + item + move] for move in range(4)], axis=0)
                    for item in range(merged)
                ],
                axis=1,
            )
            preact = lax.dot_general(across, weights[...], (((0,), (0,)), ((), ())), preferred_element_type=F32)
            square, curve, half = gelu_parts(preact)
            active = half + half * curve
            sums = sums + jnp.sum(active.reshape(merged * LANES // 8, 8, active.shape[1]), axis=0)
            slope = (0.5 + 0.5 * curve) + (half * (1.0 - curve * curve)) * (ROOT + (3.0 * ROOT * CUBIC) * square)
            total[...] += jnp.dot(across, slope.astype(BF16), preferred_element_type=F32)
        pool[...] = sums
        return 0

    lax.fori_loop(0, lows // merged, step, 0)
    line = jnp.sum(pool[...], axis=0, keepdims=True)
    column = jnp.broadcast_to(line, (LANES, line.shape[1])).T
    latent = jnp.sum(column * heads.astype(F32), axis=0, keepdims=True)
    payload[...] = jnp.zeros_like(payload)
    for device in range(payload.shape[0]):
        target = device // groups % share
        payload[device, 0:1, :] = latent
        payload[device, 1:2, 0:rows] = line[:, target * rows : (target + 1) * rows]
    split[...] = swap_units(total[...], 8, 2).T.reshape(share, rows, wide)
    for turn in range(share):
        grads[turn][...] = split[grp_pos ^ turn]


def odd_rows(even, following):
    lane = lax.broadcasted_iota(jnp.int32, even.shape, 1)
    return jnp.where(lane % 16 < 8, pltpu.roll(even, LANES - 8, 1), pltpu.roll(following, 8, 1))


def encode_kernel(groups, scalars, flat, weights, out, tall, near):
    tile = out.shape[0]
    lows = flat.shape[0] - 4

    @pl.when(pl.program_id(0) == 0)
    def _():
        me = scalars[0]
        for index in range(lows + 4):
            tall[index * LANES : (index + 1) * LANES, :] = flat[index].astype(F32).T
        inner = min(2 * lows, LANES)
        parts = LANES // inner
        highs = LANES // groups
        end = 8 + highs * lows
        near[0:8, :] = jnp.zeros((8, LANES), F32)
        near[end:, :] = jnp.zeros((16, LANES), F32)
        for item in range(highs):
            high = me * highs + item
            lane = (high % parts) * inner + high // parts
            if item == 0:
                near[6:8, :] = tall[pl.ds(lane, 2, stride=LANES), :]
            near[8 + item * lows : 8 + (item + 1) * lows, :] = tall[pl.ds(2 * LANES + lane, lows, stride=LANES), :]
            if item == highs - 1:
                near[end : end + 2, :] = tall[pl.ds((lows + 2) * LANES + lane, 2, stride=LANES), :]

    at = pl.multiple_of(pl.program_id(0) * tile, tile)
    window = near[pl.ds(at, tile + 24), :]
    even = window[: tile + 16]
    shifted = odd_rows(even, window[1 : tile + 17])
    sums = None
    for rows in (even, shifted):
        preact = jnp.dot(stack_rows(rows, tile), weights[...], preferred_element_type=F32)
        _, curve, half = gelu_parts(preact)
        active = half + half * curve
        sums = active if sums is None else sums + active
    out[...] = (sums * 0.5).astype(BF16)


def loss_kernel(groups, share, full_len, listed, ready, scalars, arrived, projection, loss, factors, grad):
    branch, grp_pos = scalars[1], scalars[2]
    batch = share
    exact = lax.Precision.HIGHEST
    latents = []
    for side in range(2):
        lines = []
        for item in range(batch):
            base = (side * share + item) * groups
            line = arrived[base, 0:1, :]
            for turn in range(1, groups):
                line = line + arrived[base + turn, 0:1, :]
            lines.append(line * (1.0 / full_len))
        latents.append(jnp.concatenate(lines, axis=0))
    scale = [lax.rsqrt(jnp.sum(latent * latent, axis=1, keepdims=True) + 1e-06) for latent in latents]
    embs = [latent * factor for latent, factor in zip(latents, scale)]
    logits = lax.dot_general(embs[0], embs[1], (((1,), (1,)), ((), ())), precision=exact, preferred_element_type=F32) / TAU
    row = lax.broadcasted_iota(jnp.int32, logits.shape, 0)
    col = lax.broadcasted_iota(jnp.int32, logits.shape, 1)
    target = jnp.zeros_like(logits)
    for item in range(batch):
        target = jnp.where((row == item) & (col == scalars[3 + 2 * listed + item]), 1.0, target)
    power = jnp.exp(logits)
    row_sum = jnp.sum(power, axis=1, keepdims=True)
    col_sum = jnp.sum(power, axis=0, keepdims=True)
    value = (
        jnp.sum(jnp.log(row_sum), axis=(0, 1), keepdims=True)
        + jnp.sum(jnp.log(col_sum), axis=(0, 1), keepdims=True)
        - 2.0 * jnp.sum(target * logits, axis=(0, 1), keepdims=True)
    ) / (2.0 * batch)
    loss[0, 0] = jnp.sum(value)
    slope = (power / row_sum + power / col_sum - 2.0 * target) * (LOSS_SCALE / (2.0 * batch * TAU))
    emb_grads = [
        lax.dot_general(slope, embs[1], (((1,), (0,)), ((), ())), precision=exact, preferred_element_type=F32),
        lax.dot_general(slope.T, embs[0], (((1,), (0,)), ((), ())), precision=exact, preferred_element_type=F32),
    ]
    own = []
    for side in range(2):
        inner = jnp.sum(emb_grads[side] * embs[side], axis=1, keepdims=True)
        own.append(scale[side] * (emb_grads[side] - embs[side] * inner))
    latent_grad = jnp.where(branch == 0, own[0], own[1])
    rows = factors.shape[0]
    if ready:
        weights = projection[...].astype(F32)
    else:
        start = pl.multiple_of((grp_pos * groups + scalars[0]) * rows, 16)
        weights = projection[pl.ds(start, rows), :].astype(F32)
    lane = lax.broadcasted_iota(jnp.int32, (rows, LANES), 1)
    spread = jnp.zeros((rows, LANES), F32)
    for item in range(batch):
        column = jnp.sum(weights * latent_grad[item : item + 1, :], axis=1, keepdims=True) * (1.0 / full_len)
        spread = jnp.where(lane == item, column, spread)
    factors[...] = spread
    for turn in range(groups):
        lines = [arrived[(branch * share + item) * groups + turn, 1:2, :] for item in range(batch)]
        lines = lines + [jnp.zeros((8 - batch % 8, LANES), F32)] if batch % 8 else lines
        sums = jnp.concatenate(lines, axis=0).T * (1.0 / full_len)
        value = sums[:, 0:1] * latent_grad[0:1, :]
        for item in range(1, batch):
            value = value + sums[:, item : item + 1] * latent_grad[item : item + 1, :]
        grad[turn * rows : (turn + 1) * rows, :] = value[:rows]


def combine_kernel(share, scalars, factors, *refs):
    pieces, out = refs[:share], refs[share]
    grp_pos = scalars[2]
    values = factors[...]
    lane = lax.broadcasted_iota(jnp.int32, values.shape, 1)
    result = None
    for turn in range(share):
        column = jnp.sum(jnp.where(lane == (grp_pos ^ turn), values, 0.0), axis=1, keepdims=True)
        term = column * pieces[turn][...]
        result = term if result is None else result + term
    out[...] = result


def assemble(slots, groups, low_count, seq_pos, branch):
    order = jnp.arange(groups, dtype=jnp.int32) ^ seq_pos
    held = jnp.stack(slots).reshape(2, groups, low_count // 2, 2, -1, LANES)[:, order]
    held = jnp.where(branch == 0, held, held[::-1])
    held = jnp.transpose(held, (2, 3, 0, 1, 4, 5)).reshape(low_count // 2, 2, 8, 8, LANES)
    return jnp.transpose(held, (0, 2, 1, 3, 4)).reshape(-1, LANES)


def body(series, time_blocks, freq_blocks, positives, conv_weight, proj_weight):
    groups = lax.axis_size("seq")
    share = lax.axis_size("grp")
    sides = lax.axis_size("pair")
    seq_pos = lax.axis_index("seq")
    branch = lax.axis_index("pair")
    grp_pos = lax.axis_index("grp")
    samples, length, own_chan = series.shape
    assert samples == 1 and sides == 2 and 4 * own_chan == LANES
    full_len = length * groups
    hidden, width = conv_weight.shape[1:]
    emb_dim = proj_weight.shape[2]
    chans = own_chan // groups
    low_count = full_len // LANES
    lows = low_count // 2
    rows = hidden // (share * groups)
    listed = time_blocks.shape[1]
    ready = chans != 8 or rows % 16 != 0
    places = jnp.stack([seq_pos, branch, grp_pos]).astype(jnp.int32)
    scalars = jnp.concatenate([places, time_blocks[0], freq_blocks[0], positives])
    weight, heads = conv_weight[0], proj_weight[0]
    picked, own_heads, mid_heads = weight, heads, heads
    if ready:
        picked = lax.dynamic_index_in_dim(weight.reshape(share, groups, rows, width), seq_pos, 1, keepdims=False)
        picked = picked.reshape(share * rows, width)
        mid_heads = lax.dynamic_index_in_dim(heads.reshape(share, groups, rows, emb_dim), seq_pos, 1, keepdims=False)
        mid_heads = mid_heads.reshape(share * rows, emb_dim)
        own_heads = lax.dynamic_slice_in_dim(heads, (grp_pos * groups + seq_pos) * rows, rows, 0)

    piece = jax.ShapeDtypeStruct((chans, length), F32)
    with jax.named_scope("arrange"):
        pieces = call(arrange_kernel, [piece] * groups, [SMEM, VMEM], moved=5 * 10**5)(
            scalars, series[0].T.reshape(groups, chans, length)
        )
    pieces = [pieces[0]] + [
        lax.ppermute(pieces[turn], "seq", [(i, i ^ turn) for i in range(groups)]) for turn in range(1, groups)
    ]
    tables = [jnp.asarray(table) for table in fourier_tables(full_len)]
    with jax.named_scope("prepare"):
        weights, part_weights, *tables = call(
            functools.partial(prepare_kernel, groups, share, ready),
            [jax.ShapeDtypeStruct((width, hidden), BF16), jax.ShapeDtypeStruct((width, share * rows), BF16)]
            + [jax.ShapeDtypeStruct(table.shape, table.dtype) for table in tables],
            [SMEM] + [VMEM] * 6,
            flops=10**8,
            moved=3 * 10**6,
            room=24,
        )(scalars, weight, picked, *tables)
    wire = jax.ShapeDtypeStruct((chans * low_count, LANES), BF16)
    with jax.named_scope("fourier"):
        own, pay = call(
            functools.partial(fourier_kernel, groups, full_len, length // 8, listed),
            [wire, wire],
            [SMEM] + [VMEM] * (4 + groups),
            [
                pltpu.VMEM((groups, chans, length), F32),
                pltpu.VMEM((chans * low_count, LANES), F32),
                pltpu.VMEM((chans * low_count, LANES), F32),
                pltpu.VMEM((chans * low_count, LANES), F32),
                pltpu.VMEM((chans * low_count, LANES), F32),
            ],
            flops=10**9,
            moved=2 * 10**6,
        )(scalars, *tables, *pieces)

    slots = [None] * (2 * groups)
    for flip in range(2):
        for turn in range(0, groups, 2):
            block = pay if flip else own
            if flip or turn:
                pairs = [
                    (p * groups + i, (p ^ flip) * groups + (i ^ turn)) for p in range(2) for i in range(groups)
                ]
                block = lax.ppermute(block, ("pair", "seq"), pairs)
            slots[flip * groups + turn] = block
    for flip in range(2):
        for turn in range(0, groups, 2):
            slots[flip * groups + turn + 1] = lax.ppermute(
                slots[flip * groups + turn], "seq", [(i, i ^ 1) for i in range(groups)]
            )
    if ready:
        slots = [assemble(slots, groups, low_count, seq_pos, branch)]

    devices = sides * share * groups
    tiles = jax.ShapeDtypeStruct((lows + 4, LANES, LANES), BF16)
    with jax.named_scope("slope"):
        *grads, payload, flat = call(
            functools.partial(slope_kernel, groups, ready, 8),
            [jax.ShapeDtypeStruct((rows, width), F32)] * share
            + [jax.ShapeDtypeStruct((devices, 8, LANES), F32), tiles],
            [SMEM] + [VMEM] * (2 + len(slots)),
            [
                pltpu.VMEM((lows + 4, LANES, LANES), BF16),
                pltpu.VMEM((width, share * rows), F32),
                pltpu.VMEM((8, share * rows), F32),
                pltpu.VMEM((share, rows, width), F32),
            ],
            flops=4 * full_len * share * rows * width,
            moved=4 * 10**6,
            room=20 + 8 * (low_count // LANES),
        )(scalars, part_weights, mid_heads, *slots)
    grads = [grads[0]] + [
        lax.ppermute(grads[turn], "grp", [(i, i ^ turn) for i in range(share)]) for turn in range(1, share)
    ]
    arrived = lax.all_to_all(payload, ("pair", "grp", "seq"), split_axis=0, concat_axis=0, tiled=True)
    enc_tile = 256
    near_len = length // 2
    with jax.named_scope("encode"):
        encoded = pl.pallas_call(
            functools.partial(encode_kernel, groups),
            out_shape=jax.ShapeDtypeStruct((near_len, hidden), BF16),
            grid=(near_len // enc_tile,),
            in_specs=[SMEM, VMEM, VMEM],
            out_specs=pl.BlockSpec((enc_tile, hidden), lambda i: (i, 0)),
            scratch_shapes=[
                pltpu.VMEM(((lows + 4) * LANES, LANES), F32),
                pltpu.VMEM((near_len + 24, LANES), F32),
            ],
            compiler_params=pltpu.CompilerParams(vmem_limit_bytes=(20 + 12 * (low_count // LANES)) * 1024 * 1024),
            cost_estimate=pl.CostEstimate(
                flops=2 * length * hidden * width, bytes_accessed=4 * 10**6, transcendentals=length * hidden
            ),
        )(scalars, flat, weights)
    with jax.named_scope("loss"):
        loss, factors, proj_share = call(
            functools.partial(loss_kernel, groups, share, full_len, listed, ready),
            [
                jax.ShapeDtypeStruct((1, 1), F32),
                jax.ShapeDtypeStruct((rows, LANES), F32),
                jax.ShapeDtypeStruct((groups * rows, emb_dim), F32),
            ],
            [SMEM] + [VMEM] * 2,
            flops=10**7,
            moved=10**6,
            out_specs=[SMEM, VMEM, VMEM],
        )(scalars, arrived, own_heads)
    with jax.named_scope("combine"):
        conv_share = call(
            functools.partial(combine_kernel, share),
            jax.ShapeDtypeStruct((rows, width), F32),
            [SMEM] + [VMEM] * (1 + share),
            flops=10**6,
            moved=5 * 10**5,
        )(scalars, factors, *grads)
    return (encoded[None, None], loss.reshape(()), conv_share[None], proj_share[None])


def solution(mesh):
    in_specs = (
        P("grp", "seq", "pair"),
        P("grp", None),
        P("grp", None),
        P(),
        P("pair", None, None),
        P("pair", None, None),
    )
    out_specs = (
        P("pair", "grp", "seq", None),
        P(),
        P("pair", ("grp", "seq"), None),
        P("pair", "grp", None),
    )
    return jax.shard_map(body, mesh=mesh, in_specs=in_specs, out_specs=out_specs, check_vma=False)
```

```python
import functools
import math

import jax
import jax.numpy as jnp
import numpy as np
from jax import lax
from jax.experimental import pallas as pl
from jax.experimental.pallas import tpu as pltpu
from jax.sharding import PartitionSpec as P

TAU = 0.2
LOSS_SCALE = 256.0
LANES = 128
ROOT = math.sqrt(2.0 / math.pi)
CUBIC = 0.044715
F32 = jnp.float32
BF16 = jnp.bfloat16

VMEM = pl.BlockSpec(memory_space=pltpu.VMEM)
SMEM = pl.BlockSpec(memory_space=pltpu.SMEM)
HBM = pl.BlockSpec(memory_space=pltpu.HBM)


def call(kernel, out_shape, in_specs, scratch=(), flops=0, moved=0, room=16, out_specs=None):
    single = not isinstance(out_shape, (list, tuple))
    return pl.pallas_call(
        kernel,
        out_shape=out_shape,
        in_specs=in_specs,
        out_specs=out_specs or (VMEM if single else [VMEM] * len(out_shape)),
        scratch_shapes=list(scratch),
        compiler_params=pltpu.CompilerParams(vmem_limit_bytes=room * 1024 * 1024),
        cost_estimate=pl.CostEstimate(flops=flops, bytes_accessed=moved, transcendentals=0),
    )


def lane_order(low_count):
    inner = min(low_count, LANES)
    parts = LANES // inner
    lane = np.arange(LANES)
    return parts * (lane % inner) + lane // inner


def fourier_tables(full_len):
    low_count = full_len // LANES
    first = np.arange(low_count)
    rest = np.arange(LANES)
    second = lane_order(low_count)
    angle = (first[:, None] * first[None, :] % low_count) * (2.0 * np.pi / low_count)
    stage_one = np.concatenate([np.cos(angle), -np.sin(angle)], axis=0)
    turn = (first[:, None] * rest[None, :] % full_len) * (2.0 * np.pi / full_len)
    angle = (rest[:, None] * second[None, :] % LANES) * (2.0 * np.pi / LANES)
    cos, sin = np.cos(angle), np.sin(angle)
    stage_two = np.block([[cos, -sin], [sin, cos]])
    wide = np.zeros((2 * low_count, 2 * LANES))
    wide[:, :low_count] = stage_one
    turns = np.concatenate([np.cos(turn), np.sin(turn)], axis=1)
    return np.concatenate([stage_two, turns, wide], axis=0).astype(np.float32)


def arrange_kernel(series, *refs):
    *pieces, done = refs
    me = lax.axis_index("seq")
    copies = [pltpu.make_async_copy(series.at[me ^ turn], piece, done.at[turn]) for turn, piece in enumerate(pieces)]
    for copy in copies:
        copy.start()
    for copy in copies:
        copy.wait()


def high_low(values):
    high = values.astype(BF16)
    return high, (values - high.astype(F32)).astype(BF16)


def keep_lanes(scalars, first, number, low_count, block_len):
    lane = lax.broadcasted_iota(jnp.int32, (8, LANES), 1)
    inner = min(low_count, LANES)
    parts = LANES // inner
    high = parts * (lane % inner) + lane // inner
    block = high * low_count // block_len
    keep = jnp.ones((8, LANES), F32)
    for entry in range(first, first + number):
        keep = jnp.where(block == scalars[entry], 0.0, keep)
    return keep[0:1]


def fourier_kernel(
    groups, full_len, block_len, listed, scalars, stage_one, turns, stage_two, *refs
):
    pieces = refs[:groups]
    own, pay, gathered, steps, mags, views, wire = refs[groups:]
    me, branch = scalars[0], scalars[1]
    low_count = full_len // LANES
    chans, length = pieces[0].shape
    tops = length // LANES
    for turn in range(groups):
        gathered[turn] = pieces[turn][...]
    for source in range(groups):
        block = gathered[source ^ me]
        for top in range(tops):
            at = (source * tops + top) * chans
            steps[at : at + chans, :] = block[:, top * LANES : (top + 1) * LANES]
    columns = [steps[pl.ds(chan, low_count, stride=chans), :] for chan in range(chans)]
    high, low = high_low(jnp.concatenate(columns, axis=1))
    first = jnp.dot(stage_one[...], jnp.concatenate([high, high, low], axis=0), preferred_element_type=F32)
    cos, sin = turns[:, :LANES], turns[:, LANES:]
    turned = []
    for chan in range(chans):
        part = first[:, chan * LANES : (chan + 1) * LANES]
        part_re, part_im = part[:low_count], part[low_count:]
        turned.append(jnp.concatenate([part_re * cos + part_im * sin, part_im * cos - part_re * sin], axis=1))
    high, low = high_low(jnp.concatenate(turned, axis=0))
    second = jnp.dot(jnp.concatenate([high, high, low], axis=1), stage_two[...], preferred_element_type=F32)
    spec_re, spec_im = second[:, :LANES], second[:, LANES:]
    magnitude = jnp.sqrt(1.0 + (spec_re * spec_re + spec_im * spec_im) * (1.0 / full_len))
    mags[...] = magnitude.astype(BF16).astype(F32) * keep_lanes(scalars, 3 + listed, listed, low_count, block_len)
    time_keep = keep_lanes(scalars, 3, listed, low_count, block_len)
    for chan in range(chans):
        if low_count < LANES:
            turned_steps = columns[chan].T
            view = jnp.concatenate(
                [turned_steps[part * low_count : (part + 1) * low_count] for part in range(LANES // low_count)], axis=1
            )
        else:
            parts = low_count // LANES
            view = jnp.concatenate(
                [steps[pl.ds(chan + chans * part, LANES, stride=chans * parts), :].T for part in range(parts)], axis=0
            )
        views[chan * low_count : (chan + 1) * low_count, :] = view * time_keep

    def spread(held, out):
        for low in range(low_count):
            wire[chans * low : chans * (low + 1), :] = held[pl.ds(low, chans, stride=low_count), :]
        out[...] = wire[...].astype(BF16)

    @pl.when(branch == 0)
    def _():
        spread(views, own)
        spread(mags, pay)

    @pl.when(branch != 0)
    def _():
        spread(mags, own)
        spread(views, pay)


def gelu_parts(half):
    square = half * half
    return square, 1.0 + jnp.tanh(half * (2.0 * ROOT + (8.0 * ROOT * CUBIC) * square))


def stack_rows(window, count):
    return jnp.concatenate([window[6 + shift : 6 + shift + count] for shift in range(4)], axis=1).astype(BF16)


def shift_high(tile, low_count, step):
    inner = min(low_count, LANES)
    lane = lax.broadcasted_iota(jnp.int32, tile.shape, 1)
    if step < 0:
        moved = jnp.where(lane < inner, pltpu.roll(tile, (inner + 1) % LANES, 1), pltpu.roll(tile, inner % LANES, 1))
        return jnp.where(lane == 0, 0.0, moved)
    back = LANES - inner
    moved = jnp.where(lane < back, pltpu.roll(tile, back, 1), pltpu.roll(tile, (back - 1) % LANES, 1))
    return jnp.where(lane == LANES - 1, 0.0, moved)


def swap_units(values, outer, inner):
    unit = outer * inner * 8
    blocks = []
    for start in range(0, values.shape[0], unit):
        for second in range(inner):
            for first in range(outer):
                at = start + (first * inner + second) * 8
                blocks.append(values[at : at + 8])
    return jnp.concatenate(blocks, axis=0)


def prepare_kernel(groups, share, low_count, scalars, weight, picked, table, full, part, stage_one, turns, stage_two):
    me = scalars[0]
    full[...] = swap_units(0.5 * weight[...].astype(F32).T, 2, 8).astype(BF16)
    if picked is not None:
        rows = picked[...]
    else:
        size = weight.shape[0] // (share * groups)
        starts = [pl.multiple_of((group * groups + me) * size, 16) for group in range(share)]
        rows = jnp.concatenate([weight[pl.ds(start, size), :] for start in starts], axis=0)
    part[...] = swap_units(0.5 * rows.astype(F32).T, 2, 8).astype(BF16)
    high, low = high_low(table[: 2 * LANES])
    stage_two[...] = jnp.concatenate([high, low, high], axis=0)
    turns[...] = table[2 * LANES : 2 * LANES + low_count]
    high, low = high_low(table[2 * LANES + low_count :, :low_count])
    stage_one[...] = jnp.concatenate([high, low, high], axis=1)


def prepare_whole(kernel, scalars, weight, *refs):
    kernel(scalars, weight, None, *refs)


def slope_kernel(groups, ready, merged, small, scalars, weights, projection, *refs):
    count = 1 if ready else 2 * groups
    slots = refs[:count]
    grads = refs[count:-6]
    payload, flat, odd, total, pool, split = refs[-6:]
    me, branch, grp_pos = scalars[0], scalars[1], scalars[2]
    lows = flat.shape[0] - 4
    low_count = 2 * lows
    share = len(grads)
    wide = 4 * LANES
    rows = grads[0].shape[0]
    if ready:
        flat[2 : 2 + lows] = slots[0][...].reshape(lows, LANES, LANES)
        heads = projection[...]
    else:
        for flip in range(2):
            for turn in range(groups):
                at = pl.multiple_of(((branch ^ flip) * groups + (me ^ turn)) * 16, 16)
                flat[2 : 2 + lows, pl.ds(at, 16), :] = slots[flip * groups + turn][...].reshape(lows, 16, LANES)
        starts = [pl.multiple_of((group * groups + me) * rows, 16) for group in range(share)]
        heads = jnp.concatenate([projection[pl.ds(start, rows), :] for start in starts], axis=0)
    for edge in range(2):
        flat[edge] = shift_high(flat[lows + edge].astype(F32), low_count, -1).astype(BF16)
        flat[lows + 2 + edge] = shift_high(flat[2 + edge].astype(F32), low_count, 1).astype(BF16)
    current = flat[0].astype(F32).reshape(8, 2, 8, LANES)
    for index in range(lows + 3):
        following = flat[index + 1].astype(F32).reshape(8, 2, 8, LANES)
        mixed = jnp.concatenate([current[:, 1:2], following[:, 0:1]], axis=1)
        odd[index] = mixed.reshape(LANES, LANES).astype(BF16)
        current = following
    total[...] = jnp.zeros_like(total)
    pool[...] = jnp.zeros_like(pool)

    def step(index, _):
        first = index * merged
        sums = pool[...]
        for source in (flat, odd):
            patches, slopes = [], []
            for item in range(0, merged, small):
                stacks = [
                    jnp.concatenate([source[first + item + at + move] for move in range(4)], axis=0)
                    for at in range(small)
                ]
                across = jnp.concatenate(stacks, axis=1)
                half = lax.dot_general(across, weights[...], (((0,), (0,)), ((), ())), preferred_element_type=F32)
                square, curve = gelu_parts(half)
                active = half * curve
                sums = sums + jnp.sum(active.reshape(small * LANES // 8, 8, active.shape[1]), axis=0)
                inner = half * (2.0 - curve) * (ROOT + (12.0 * ROOT * CUBIC) * square)
                slopes.append((curve * (0.5 + inner)).astype(BF16))
                patches.append(across)
            total[...] += jnp.dot(
                jnp.concatenate(patches, axis=1), jnp.concatenate(slopes, axis=0), preferred_element_type=F32
            )
        pool[...] = sums
        return 0

    lax.fori_loop(0, lows // merged, step, 0)
    line = jnp.sum(pool[...], axis=0, keepdims=True)
    column = jnp.broadcast_to(line, (LANES, line.shape[1])).T
    latent = jnp.sum(column * heads.astype(F32), axis=0, keepdims=True)
    payload[...] = jnp.zeros_like(payload)
    for device in range(payload.shape[0]):
        target = device // groups % share
        payload[device, 0:1, :] = latent
        payload[device, 1:2, 0:rows] = line[:, target * rows : (target + 1) * rows]
    split[...] = swap_units(total[...], 8, 2).T.reshape(share, rows, wide)
    for turn in range(share):
        grads[turn][...] = split[grp_pos ^ turn]


def odd_rows(even, following):
    lane = lax.broadcasted_iota(jnp.int32, even.shape, 1)
    return jnp.where(lane % 16 < 8, pltpu.roll(even, LANES - 8, 1), pltpu.roll(following, 8, 1))


def encode_kernel(groups, chunk, scalars, flat, weights, out, tall, near, patches):
    count = out.shape[0]
    lows = flat.shape[0] - 4

    @pl.when(pl.program_id(0) == 0)
    def _():
        me = scalars[0]
        for index in range(lows + 4):
            tall[index * LANES : (index + 1) * LANES, :] = flat[index].astype(F32).T
        inner = min(2 * lows, LANES)
        parts = LANES // inner
        highs = LANES // groups
        end = 8 + highs * lows
        near[0:8, :] = jnp.zeros((8, LANES), F32)
        near[end:, :] = jnp.zeros((16, LANES), F32)
        for item in range(highs):
            high = me * highs + item
            lane = (high % parts) * inner + high // parts
            if item == 0:
                near[6:8, :] = tall[pl.ds(lane, 2, stride=LANES), :]
            near[8 + item * lows : 8 + (item + 1) * lows, :] = tall[pl.ds(2 * LANES + lane, lows, stride=LANES), :]
            if item == highs - 1:
                near[end : end + 2, :] = tall[pl.ds((lows + 2) * LANES + lane, 2, stride=LANES), :]
        for start in range(0, count, LANES):
            window = near[start : start + LANES + 24, :]
            even = window[: LANES + 16]
            patches[0, start : start + LANES, :] = stack_rows(even, LANES)
            patches[1, start : start + LANES, :] = stack_rows(odd_rows(even, window[1 : LANES + 17]), LANES)

    for start in range(0, count, chunk):
        sums = None
        for parity in range(2):
            half = jnp.dot(patches[parity, start : start + chunk], weights[...], preferred_element_type=F32)
            active = half * gelu_parts(half)[1]
            sums = active if sums is None else sums + active
        out[start : start + chunk, :] = (sums * 0.5).astype(BF16)


def loss_kernel(groups, share, full_len, listed, ready, scalars, arrived, projection, *refs):
    pieces, (loss, out, grad) = refs[:share], refs[share:]
    branch, grp_pos = scalars[1], scalars[2]
    batch = share
    latents = []
    for side in range(2):
        lines = []
        for item in range(batch):
            base = (side * share + item) * groups
            lines.append(jnp.sum(arrived[base : base + groups, 0:1, :], axis=0) * (1.0 / full_len))
        latents.append(jnp.concatenate(lines, axis=0))
    scale = [lax.rsqrt(jnp.sum(latent * latent, axis=1, keepdims=True) + 1e-06) for latent in latents]
    embs = [latent * factor for latent, factor in zip(latents, scale)]
    row = lax.broadcasted_iota(jnp.int32, (batch, LANES), 0)
    lane = lax.broadcasted_iota(jnp.int32, (batch, LANES), 1)
    logits = jnp.zeros((batch, LANES), F32)
    target = jnp.zeros((batch, LANES), F32)
    for item in range(batch):
        column = jnp.sum(embs[0] * embs[1][item : item + 1], axis=1, keepdims=True) / TAU
        logits = jnp.where(lane == item, column, logits)
        target = jnp.where((row == item) & (lane == scalars[3 + 2 * listed + item]), 1.0, target)
    inside = lane < batch
    power = jnp.where(inside, jnp.exp(logits), 0.0)
    row_sum = jnp.sum(power, axis=1, keepdims=True)
    col_sum = jnp.where(inside[0:1], jnp.sum(power, axis=0, keepdims=True), 1.0)
    value = jnp.log(col_sum) + jnp.sum(
        jnp.where(lane == 0, jnp.log(row_sum), 0.0) - 2.0 * target * logits, axis=0, keepdims=True
    )
    loss[0, 0] = jnp.sum(value) / (2.0 * batch)
    slope = (power / row_sum + power / col_sum - 2.0 * target) * (LOSS_SCALE / (2.0 * batch * TAU))
    emb_grads = [jnp.zeros((batch, LANES), F32), []]
    for item in range(batch):
        column = slope[:, item : item + 1]
        emb_grads[0] = emb_grads[0] + column * embs[1][item : item + 1]
        emb_grads[1].append(jnp.sum(column * embs[0], axis=0, keepdims=True))
    emb_grads[1] = jnp.concatenate(emb_grads[1], axis=0)
    own = []
    for side in range(2):
        inner = jnp.sum(emb_grads[side] * embs[side], axis=1, keepdims=True)
        own.append(scale[side] * (emb_grads[side] - embs[side] * inner))
    latent_grad = jnp.where(branch == 0, own[0], own[1]) * (1.0 / full_len)
    rows = out.shape[0]
    if ready:
        weights = projection[...].astype(F32)
    else:
        start = pl.multiple_of((grp_pos * groups + scalars[0]) * rows, 16)
        weights = projection[pl.ds(start, rows), :].astype(F32)
    spread = jnp.zeros((rows, LANES), F32)
    lane = lax.broadcasted_iota(jnp.int32, (rows, LANES), 1)
    for item in range(batch):
        column = jnp.sum(weights * latent_grad[item : item + 1, :], axis=1, keepdims=True)
        spread = jnp.where(lane == item, column, spread)
    for turn in range(groups):
        lines = [arrived[(branch * share + item) * groups + turn, 1:2, :] for item in range(batch)]
        if batch % 8:
            lines.append(jnp.zeros((8 - batch % 8, LANES), F32))
        sums = jnp.concatenate(lines, axis=0).T
        value = sums[:, 0:1] * latent_grad[0:1, :]
        for item in range(1, batch):
            value = value + sums[:, item : item + 1] * latent_grad[item : item + 1, :]
        grad[turn * rows : (turn + 1) * rows, :] = value[:rows]
    result = None
    for turn in range(share):
        column = jnp.sum(jnp.where(lane == (grp_pos ^ turn), spread, 0.0), axis=1, keepdims=True)
        term = column * pieces[turn][...]
        result = term if result is None else result + term
    out[...] = result


def assemble(slots, groups, low_count, seq_pos, branch):
    order = jnp.arange(groups, dtype=jnp.int32) ^ seq_pos
    held = jnp.stack(slots).reshape(2, groups, low_count // 2, 2, -1, LANES)[:, order]
    held = jnp.where(branch == 0, held, held[::-1])
    held = jnp.transpose(held, (2, 3, 0, 1, 4, 5)).reshape(low_count // 2, 2, 8, 8, LANES)
    return jnp.transpose(held, (0, 2, 1, 3, 4)).reshape(-1, LANES)


def body(series, time_blocks, freq_blocks, positives, conv_weight, proj_weight):
    groups = lax.axis_size("seq")
    share = lax.axis_size("grp")
    sides = lax.axis_size("pair")
    seq_pos = lax.axis_index("seq")
    branch = lax.axis_index("pair")
    grp_pos = lax.axis_index("grp")
    samples, length, own_chan = series.shape
    assert samples == 1 and sides == 2 and 4 * own_chan == LANES
    full_len = length * groups
    hidden, width = conv_weight.shape[1:]
    emb_dim = proj_weight.shape[2]
    chans = own_chan // groups
    low_count = full_len // LANES
    lows = low_count // 2
    rows = hidden // (share * groups)
    listed = time_blocks.shape[1]
    ready = chans != 8 or rows % 16 != 0
    places = jnp.stack([seq_pos, branch, grp_pos]).astype(jnp.int32)
    scalars = jnp.concatenate([places, time_blocks[0], freq_blocks[0], positives])
    weight, heads = conv_weight[0], proj_weight[0]
    picked, own_heads, mid_heads = weight, heads, heads
    if ready:
        picked = lax.dynamic_index_in_dim(weight.reshape(share, groups, rows, width), seq_pos, 1, keepdims=False)
        picked = picked.reshape(share * rows, width)
        mid_heads = lax.dynamic_index_in_dim(heads.reshape(share, groups, rows, emb_dim), seq_pos, 1, keepdims=False)
        mid_heads = mid_heads.reshape(share * rows, emb_dim)
        own_heads = lax.dynamic_slice_in_dim(heads, (grp_pos * groups + seq_pos) * rows, rows, 0)

    piece = jax.ShapeDtypeStruct((chans, length), F32)
    with jax.named_scope("arrange"):
        pieces = call(
            arrange_kernel,
            [piece] * groups,
            [HBM],
            [pltpu.SemaphoreType.DMA((groups,))],
            moved=5 * 10**5,
        )(series[0].T.reshape(groups, chans, length))
    pieces = [pieces[0]] + [
        lax.ppermute(pieces[turn], "seq", [(i, i ^ turn) for i in range(groups)]) for turn in range(1, groups)
    ]
    table = jnp.asarray(fourier_tables(full_len))
    with jax.named_scope("prepare"):
        kernel = functools.partial(prepare_kernel, groups, share, low_count)
        if not ready:
            kernel = functools.partial(prepare_whole, kernel)
        weights, part_weights, stage_one, turns, stage_two = call(
            kernel,
            [
                jax.ShapeDtypeStruct((width, hidden), BF16),
                jax.ShapeDtypeStruct((width, share * rows), BF16),
                jax.ShapeDtypeStruct((2 * low_count, 3 * low_count), BF16),
                jax.ShapeDtypeStruct((low_count, 2 * LANES), F32),
                jax.ShapeDtypeStruct((6 * LANES, 2 * LANES), BF16),
            ],
            [SMEM] + [VMEM] * (3 if ready else 2),
            flops=10**8,
            moved=3 * 10**6,
            room=24,
        )(*([scalars, weight, picked, table] if ready else [scalars, weight, table]))
    wire = jax.ShapeDtypeStruct((chans * low_count, LANES), BF16)
    with jax.named_scope("fourier"):
        own, pay = call(
            functools.partial(fourier_kernel, groups, full_len, length // 8, listed),
            [wire, wire],
            [SMEM] + [VMEM] * (3 + groups),
            [
                pltpu.VMEM((groups, chans, length), F32),
                pltpu.VMEM((chans * low_count, LANES), F32),
                pltpu.VMEM((chans * low_count, LANES), F32),
                pltpu.VMEM((chans * low_count, LANES), F32),
                pltpu.VMEM((chans * low_count, LANES), F32),
            ],
            flops=10**9,
            moved=2 * 10**6,
        )(scalars, stage_one, turns, stage_two, *pieces)

    slots = [None] * (2 * groups)
    for flip in (1, 0):
        for turn in range(groups - 2, -1, -2):
            block = pay if flip else own
            if flip or turn:
                pairs = [
                    (p * groups + i, (p ^ flip) * groups + (i ^ turn)) for p in range(2) for i in range(groups)
                ]
                block = lax.ppermute(block, ("pair", "seq"), pairs)
            slots[flip * groups + turn] = block
    for flip in range(2):
        for turn in range(0, groups, 2):
            slots[flip * groups + turn + 1] = lax.ppermute(
                slots[flip * groups + turn], "seq", [(i, i ^ 1) for i in range(groups)]
            )
    if ready:
        slots = [assemble(slots, groups, low_count, seq_pos, branch)]

    devices = sides * share * groups
    tiles = jax.ShapeDtypeStruct((lows + 4, LANES, LANES), BF16)
    with jax.named_scope("slope"):
        *grads, payload, flat = call(
            functools.partial(slope_kernel, groups, ready, 32, 4),
            [jax.ShapeDtypeStruct((rows, width), F32)] * share
            + [jax.ShapeDtypeStruct((devices, 2, LANES), F32), tiles],
            [SMEM] + [VMEM] * (2 + len(slots)),
            [
                pltpu.VMEM((lows + 4, LANES, LANES), BF16),
                pltpu.VMEM((width, share * rows), F32),
                pltpu.VMEM((8, share * rows), F32),
                pltpu.VMEM((share, rows, width), F32),
            ],
            flops=4 * full_len * share * rows * width,
            moved=4 * 10**6,
            room=20 + 8 * (low_count // LANES),
        )(scalars, part_weights, mid_heads, *slots)
    grads = [grads[0]] + [
        lax.ppermute(grads[turn], "grp", [(i, i ^ turn) for i in range(share)]) for turn in range(1, share)
    ]
    arrived = lax.all_to_all(payload, ("pair", "grp", "seq"), split_axis=0, concat_axis=0, tiled=True)
    near_len, columns = length // 2, 512
    with jax.named_scope("encode"):
        encoded = pl.pallas_call(
            functools.partial(encode_kernel, groups, 256),
            out_shape=jax.ShapeDtypeStruct((near_len, hidden), BF16),
            grid=(hidden // columns,),
            in_specs=[SMEM, VMEM, pl.BlockSpec((width, columns), lambda i: (0, i))],
            out_specs=pl.BlockSpec((near_len, columns), lambda i: (0, i)),
            scratch_shapes=[
                pltpu.VMEM(((lows + 4) * LANES, LANES), F32),
                pltpu.VMEM((near_len + 24, LANES), F32),
                pltpu.VMEM((2, near_len, width), BF16),
            ],
            compiler_params=pltpu.CompilerParams(vmem_limit_bytes=(20 + 12 * (low_count // LANES)) * 1024 * 1024),
            cost_estimate=pl.CostEstimate(
                flops=2 * length * hidden * width, bytes_accessed=4 * 10**6, transcendentals=length * hidden
            ),
        )(scalars, flat, weights)
    with jax.named_scope("loss"):
        loss, conv_share, proj_share = call(
            functools.partial(loss_kernel, groups, share, full_len, listed, ready),
            [
                jax.ShapeDtypeStruct((1, 1), F32),
                jax.ShapeDtypeStruct((rows, width), F32),
                jax.ShapeDtypeStruct((groups * rows, emb_dim), F32),
            ],
            [SMEM] + [VMEM] * (2 + share),
            flops=10**7,
            moved=10**6,
            out_specs=[SMEM, VMEM, VMEM],
        )(scalars, arrived, own_heads, *grads)
    return (encoded[None, None], loss.reshape(()), conv_share[None], proj_share[None])


def solution(mesh):
    in_specs = (
        P("grp", "seq", "pair"),
        P("grp", None),
        P("grp", None),
        P(),
        P("pair", None, None),
        P("pair", None, None),
    )
    out_specs = (
        P("pair", "grp", "seq", None),
        P(),
        P("pair", ("grp", "seq"), None),
        P("pair", "grp", None),
    )
    return jax.shard_map(body, mesh=mesh, in_specs=in_specs, out_specs=out_specs, check_vma=False)
```

```python
import functools
import math

import jax
import jax.numpy as jnp
import numpy as np
from jax import lax
from jax.experimental import pallas as pl
from jax.experimental.pallas import tpu as pltpu
from jax.sharding import PartitionSpec as P

TAU = 0.2
LOSS_SCALE = 256.0
LANES = 128
ROOT = math.sqrt(2.0 / math.pi)
CUBIC = 0.044715
F32 = jnp.float32
BF16 = jnp.bfloat16

VMEM = pl.BlockSpec(memory_space=pltpu.VMEM)
SMEM = pl.BlockSpec(memory_space=pltpu.SMEM)
HBM = pl.BlockSpec(memory_space=pltpu.HBM)


def call(kernel, out_shape, in_specs, scratch=(), flops=0, moved=0, room=16, out_specs=None):
    single = not isinstance(out_shape, (list, tuple))
    return pl.pallas_call(
        kernel,
        out_shape=out_shape,
        in_specs=in_specs,
        out_specs=out_specs or (VMEM if single else [VMEM] * len(out_shape)),
        scratch_shapes=list(scratch),
        compiler_params=pltpu.CompilerParams(vmem_limit_bytes=room * 1024 * 1024),
        cost_estimate=pl.CostEstimate(flops=flops, bytes_accessed=moved, transcendentals=0),
    )


def lane_order(low_count):
    inner = min(low_count, LANES)
    parts = LANES // inner
    lane = np.arange(LANES)
    return parts * (lane % inner) + lane // inner


def fourier_tables(full_len):
    low_count = full_len // LANES
    first = np.arange(low_count)
    rest = np.arange(LANES)
    second = lane_order(low_count)
    angle = (first[:, None] * first[None, :] % low_count) * (2.0 * np.pi / low_count)
    stage_one = np.concatenate([np.cos(angle), -np.sin(angle)], axis=0)
    turn = (first[:, None] * rest[None, :] % full_len) * (2.0 * np.pi / full_len)
    angle = (rest[:, None] * second[None, :] % LANES) * (2.0 * np.pi / LANES)
    cos, sin = np.cos(angle), np.sin(angle)
    stage_two = np.block([[cos, -sin], [sin, cos]])
    wide = np.zeros((2 * low_count, 2 * LANES))
    wide[:, :low_count] = stage_one
    turns = np.concatenate([np.cos(turn), np.sin(turn)], axis=1)
    return np.concatenate([stage_two, turns, wide], axis=0).astype(np.float32)


def arrange_kernel(series, *refs):
    *pieces, done = refs
    me = lax.axis_index("seq")
    copies = [pltpu.make_async_copy(series.at[me ^ turn], piece, done.at[turn]) for turn, piece in enumerate(pieces)]
    for copy in copies:
        copy.start()
    for copy in copies:
        copy.wait()


def high_low(values):
    high = values.astype(BF16)
    return high, (values - high.astype(F32)).astype(BF16)


def keep_lanes(scalars, first, number, low_count, block_len):
    lane = lax.broadcasted_iota(jnp.int32, (8, LANES), 1)
    inner = min(low_count, LANES)
    parts = LANES // inner
    high = parts * (lane % inner) + lane // inner
    block = high * low_count // block_len
    keep = jnp.ones((8, LANES), F32)
    for entry in range(first, first + number):
        keep = jnp.where(block == scalars[entry], 0.0, keep)
    return keep[0:1]


def fourier_kernel(
    groups, full_len, block_len, listed, scalars, stage_one, turns, stage_two, *refs
):
    pieces = refs[:groups]
    own, pay, gathered, steps, mags, views, wire = refs[groups:]
    me, branch = scalars[0], scalars[1]
    low_count = full_len // LANES
    chans, length = pieces[0].shape
    tops = length // LANES
    for turn in range(groups):
        gathered[turn] = pieces[turn][...]
    for source in range(groups):
        block = gathered[source ^ me]
        for top in range(tops):
            at = (source * tops + top) * chans
            steps[at : at + chans, :] = block[:, top * LANES : (top + 1) * LANES]
    columns = [steps[pl.ds(chan, low_count, stride=chans), :] for chan in range(chans)]
    high, low = high_low(jnp.concatenate(columns, axis=1))
    first = jnp.dot(stage_one[...], jnp.concatenate([high, high, low], axis=0), preferred_element_type=F32)
    cos, sin = turns[:, :LANES], turns[:, LANES:]
    turned = []
    for chan in range(chans):
        part = first[:, chan * LANES : (chan + 1) * LANES]
        part_re, part_im = part[:low_count], part[low_count:]
        turned.append(jnp.concatenate([part_re * cos + part_im * sin, part_im * cos - part_re * sin], axis=1))
    high, low = high_low(jnp.concatenate(turned, axis=0))
    second = jnp.dot(jnp.concatenate([high, high, low], axis=1), stage_two[...], preferred_element_type=F32)
    spec_re, spec_im = second[:, :LANES], second[:, LANES:]
    magnitude = jnp.sqrt(1.0 + (spec_re * spec_re + spec_im * spec_im) * (1.0 / full_len))
    mags[...] = magnitude.astype(BF16).astype(F32) * keep_lanes(scalars, 3 + listed, listed, low_count, block_len)
    time_keep = keep_lanes(scalars, 3, listed, low_count, block_len)
    for chan in range(chans):
        if low_count < LANES:
            turned_steps = columns[chan].T
            view = jnp.concatenate(
                [turned_steps[part * low_count : (part + 1) * low_count] for part in range(LANES // low_count)], axis=1
            )
        else:
            parts = low_count // LANES
            view = jnp.concatenate(
                [steps[pl.ds(chan + chans * part, LANES, stride=chans * parts), :].T for part in range(parts)], axis=0
            )
        views[chan * low_count : (chan + 1) * low_count, :] = view * time_keep

    def spread(held, out):
        for low in range(low_count):
            wire[chans * low : chans * (low + 1), :] = held[pl.ds(low, chans, stride=low_count), :]
        out[: wire.shape[0], :] = wire[...].astype(BF16)
        if out.shape[0] > wire.shape[0]:
            out[wire.shape[0] :, :] = jnp.zeros((out.shape[0] - wire.shape[0], LANES), BF16)

    @pl.when(branch == 0)
    def _():
        spread(views, own)
        spread(mags, pay)

    @pl.when(branch != 0)
    def _():
        spread(mags, own)
        spread(views, pay)


def gelu_parts(half):
    square = half * half
    return square, 1.0 + jnp.tanh(half * (2.0 * ROOT + (8.0 * ROOT * CUBIC) * square))


def stack_rows(window, count):
    return jnp.concatenate([window[6 + shift : 6 + shift + count] for shift in range(4)], axis=1).astype(BF16)


def shift_high(tile, low_count, step):
    inner = min(low_count, LANES)
    lane = lax.broadcasted_iota(jnp.int32, tile.shape, 1)
    if step < 0:
        moved = jnp.where(lane < inner, pltpu.roll(tile, (inner + 1) % LANES, 1), pltpu.roll(tile, inner % LANES, 1))
        return jnp.where(lane == 0, 0.0, moved)
    back = LANES - inner
    moved = jnp.where(lane < back, pltpu.roll(tile, back, 1), pltpu.roll(tile, (back - 1) % LANES, 1))
    return jnp.where(lane == LANES - 1, 0.0, moved)


def swap_units(values, outer, inner):
    unit = outer * inner * 8
    blocks = []
    for start in range(0, values.shape[0], unit):
        for second in range(inner):
            for first in range(outer):
                at = start + (first * inner + second) * 8
                blocks.append(values[at : at + 8])
    return jnp.concatenate(blocks, axis=0)


def tables_kernel(low_count, table, stage_one, turns, stage_two):
    high, low = high_low(table[: 2 * LANES])
    stage_two[...] = jnp.concatenate([high, low, high], axis=0)
    turns[...] = table[2 * LANES : 2 * LANES + low_count]
    high, low = high_low(table[2 * LANES + low_count :, :low_count])
    stage_one[...] = jnp.concatenate([high, low, high], axis=1)


def weights_kernel(groups, share, ready, scalars, weight, picked, full, part):
    me = scalars[0]
    full[...] = swap_units(0.5 * weight[...].astype(F32).T, 2, 8).astype(BF16)
    if ready:
        rows = picked[...]
    else:
        size = weight.shape[0] // (share * groups)
        starts = [pl.multiple_of((group * groups + me) * size, 16) for group in range(share)]
        rows = jnp.concatenate([weight[pl.ds(start, size), :] for start in starts], axis=0)
    part[...] = swap_units(0.5 * rows.astype(F32).T, 2, 8).astype(BF16)


def weights_whole(kernel, scalars, weight, full, part):
    kernel(scalars, weight, None, full, part)


def slope_kernel(groups, ready, merged, small, scalars, weights, projection, *refs):
    count = 1 if ready else 2 * groups
    slots = refs[:count]
    grads = refs[count:-7]
    payload, flat, odd, total, pool, sample, split = refs[-7:]
    me, branch, grp_pos = scalars[0], scalars[1], scalars[2]
    lows = flat.shape[0] - 4
    low_count = 2 * lows
    share = len(grads)
    wide = 4 * LANES
    rows = total.shape[1] // share
    if ready:
        flat[2 : 2 + lows] = slots[0][...].reshape(lows, LANES, LANES)
        heads = projection[...]
    else:
        for flip in range(2):
            for turn in range(groups):
                at = pl.multiple_of(((branch ^ flip) * groups + (me ^ turn)) * 16, 16)
                flat[2 : 2 + lows, pl.ds(at, 16), :] = slots[flip * groups + turn][: lows * 16, :].reshape(lows, 16, LANES)
        starts = [pl.multiple_of((group * groups + me) * rows, 16) for group in range(share)]
        heads = jnp.concatenate([projection[pl.ds(start, rows), :] for start in starts], axis=0)
    for edge in range(2):
        flat[edge] = shift_high(flat[lows + edge].astype(F32), low_count, -1).astype(BF16)
        flat[lows + 2 + edge] = shift_high(flat[2 + edge].astype(F32), low_count, 1).astype(BF16)
    current = flat[0].astype(F32).reshape(8, 2, 8, LANES)
    for index in range(lows + 3):
        following = flat[index + 1].astype(F32).reshape(8, 2, 8, LANES)
        mixed = jnp.concatenate([current[:, 1:2], following[:, 0:1]], axis=1)
        odd[index] = mixed.reshape(LANES, LANES).astype(BF16)
        current = following
    total[...] = jnp.zeros_like(total)
    pool[...] = jnp.zeros_like(pool)
    sample[...] = jnp.zeros_like(sample)

    def step(index, _):
        first = index * merged
        sums = pool[...]
        for source in (flat, odd):
            patches, slopes = [], []
            for item in range(0, merged, small):
                stacks = [
                    jnp.concatenate([source[first + item + at + move] for move in range(4)], axis=0)
                    for at in range(small)
                ]
                across = jnp.concatenate(stacks, axis=1)
                half = lax.dot_general(across, weights[...], (((0,), (0,)), ((), ())), preferred_element_type=F32)
                square, curve = gelu_parts(half)
                active = half * curve
                sums = sums + jnp.sum(active.reshape(small * LANES // 8, 8, active.shape[1]), axis=0)
                inner = half * (2.0 - curve) * (ROOT + (12.0 * ROOT * CUBIC) * square)
                slopes.append((curve * (0.5 + inner)).astype(BF16))
                patches.append(across)
            total[...] += jnp.dot(
                jnp.concatenate(patches, axis=1), jnp.concatenate(slopes, axis=0), preferred_element_type=F32
            )
            sample[...] += jnp.sum(slopes[0].astype(F32).reshape(small * LANES // 8, 8, -1), axis=0)
        pool[...] = sums
        return 0

    lax.fori_loop(0, lows // merged, step, 0)
    line = jnp.sum(pool[...], axis=0, keepdims=True)
    column = jnp.broadcast_to(line, (LANES, line.shape[1])).T
    latent = jnp.sum(column * heads.astype(F32), axis=0, keepdims=True)
    features = jnp.sum(flat[2 : 2 + lows].astype(F32), axis=0)
    features = jnp.sum(features, axis=1, keepdims=True).reshape(8, 2, 8, 1)
    features = (features[:, 0] + features[:, 1]).astype(BF16).astype(F32)
    column = jnp.broadcast_to(features[:, None], (8, 2, 8, 1)).reshape(LANES, 1)
    column = jnp.concatenate([column] * 4, axis=0)
    means = jnp.sum(sample[...], axis=0, keepdims=True) * (merged / (2.0 * small * LANES * lows))
    means = means.astype(BF16).astype(F32)
    split[...] = swap_units(total[...] - column * means, 8, 2).T.reshape(share, rows, wide)
    sums = jnp.broadcast_to(features.reshape(LANES // 2, 1), (LANES // 2, LANES)).T[0:1]
    fill = jnp.zeros((1, LANES - rows), F32)
    for target in range(share):
        part = slice(target * rows, (target + 1) * rows)
        lines = [
            latent,
            jnp.concatenate([line[:, part], fill], axis=1),
            jnp.concatenate([means[:, part], fill], axis=1),
            jnp.concatenate([sums, sums], axis=1),
        ]
        block = jnp.concatenate(lines, axis=0)
        for device in range(payload.shape[0]):
            if device // groups % share == target:
                payload[device] = block
    for turn, grad in enumerate(grads):
        part = split[grp_pos ^ turn]
        lines = [part[:, at : at + LANES] for at in range(0, wide, LANES)]
        if grad.shape[0] > 4 * rows:
            lines.append(jnp.zeros((grad.shape[0] - 4 * rows, LANES), F32))
        grad[...] = jnp.concatenate(lines, axis=0).astype(BF16)


def odd_rows(even, following):
    lane = lax.broadcasted_iota(jnp.int32, even.shape, 1)
    return jnp.where(lane % 16 < 8, pltpu.roll(even, LANES - 8, 1), pltpu.roll(following, 8, 1))


def encode_kernel(groups, chunk, scalars, flat, weights, out, tall, near, patches):
    count = out.shape[0]
    lows = flat.shape[0] - 4

    @pl.when(pl.program_id(0) == 0)
    def _():
        me = scalars[0]
        for index in range(lows + 4):
            tall[index * LANES : (index + 1) * LANES, :] = flat[index].astype(F32).T
        inner = min(2 * lows, LANES)
        parts = LANES // inner
        highs = LANES // groups
        end = 8 + highs * lows
        near[0:8, :] = jnp.zeros((8, LANES), F32)
        near[end:, :] = jnp.zeros((16, LANES), F32)
        for item in range(highs):
            high = me * highs + item
            lane = (high % parts) * inner + high // parts
            if item == 0:
                near[6:8, :] = tall[pl.ds(lane, 2, stride=LANES), :]
            near[8 + item * lows : 8 + (item + 1) * lows, :] = tall[pl.ds(2 * LANES + lane, lows, stride=LANES), :]
            if item == highs - 1:
                near[end : end + 2, :] = tall[pl.ds((lows + 2) * LANES + lane, 2, stride=LANES), :]
        for start in range(0, count, LANES):
            window = near[start : start + LANES + 24, :]
            even = window[: LANES + 16]
            patches[0, start : start + LANES, :] = stack_rows(even, LANES)
            patches[1, start : start + LANES, :] = stack_rows(odd_rows(even, window[1 : LANES + 17]), LANES)

    for start in range(0, count, chunk):
        sums = None
        for parity in range(2):
            half = jnp.dot(patches[parity, start : start + chunk], weights[...], preferred_element_type=F32)
            active = half * gelu_parts(half)[1]
            sums = active if sums is None else sums + active
        out[start : start + chunk, :] = (sums * 0.5).astype(BF16)


def loss_kernel(groups, share, full_len, listed, ready, scalars, arrived, projection, *refs):
    pieces, (loss, out, grad) = refs[:share], refs[share:]
    branch, grp_pos = scalars[1], scalars[2]
    batch = share
    latents = []
    for side in range(2):
        lines = []
        for item in range(batch):
            base = (side * share + item) * groups
            lines.append(jnp.sum(arrived[base : base + groups, 0:1, :], axis=0) * (1.0 / full_len))
        latents.append(jnp.concatenate(lines, axis=0))
    scale = [lax.rsqrt(jnp.sum(latent * latent, axis=1, keepdims=True) + 1e-06) for latent in latents]
    embs = [latent * factor for latent, factor in zip(latents, scale)]
    row = lax.broadcasted_iota(jnp.int32, (batch, LANES), 0)
    lane = lax.broadcasted_iota(jnp.int32, (batch, LANES), 1)
    logits = jnp.zeros((batch, LANES), F32)
    target = jnp.zeros((batch, LANES), F32)
    for item in range(batch):
        column = jnp.sum(embs[0] * embs[1][item : item + 1], axis=1, keepdims=True) / TAU
        logits = jnp.where(lane == item, column, logits)
        target = jnp.where((row == item) & (lane == scalars[3 + 2 * listed + item]), 1.0, target)
    inside = lane < batch
    power = jnp.where(inside, jnp.exp(logits), 0.0)
    row_sum = jnp.sum(power, axis=1, keepdims=True)
    col_sum = jnp.where(inside[0:1], jnp.sum(power, axis=0, keepdims=True), 1.0)
    value = jnp.log(col_sum) + jnp.sum(
        jnp.where(lane == 0, jnp.log(row_sum), 0.0) - 2.0 * target * logits, axis=0, keepdims=True
    )
    loss[0, 0] = jnp.sum(value) / (2.0 * batch)
    slope = (power / row_sum + power / col_sum - 2.0 * target) * (LOSS_SCALE / (2.0 * batch * TAU))
    emb_grads = [jnp.zeros((batch, LANES), F32), []]
    for item in range(batch):
        column = slope[:, item : item + 1]
        emb_grads[0] = emb_grads[0] + column * embs[1][item : item + 1]
        emb_grads[1].append(jnp.sum(column * embs[0], axis=0, keepdims=True))
    emb_grads[1] = jnp.concatenate(emb_grads[1], axis=0)
    own = []
    for side in range(2):
        inner = jnp.sum(emb_grads[side] * embs[side], axis=1, keepdims=True)
        own.append(scale[side] * (emb_grads[side] - embs[side] * inner))
    latent_grad = jnp.where(branch == 0, own[0], own[1]) * (1.0 / full_len)
    rows = out.shape[0]
    if ready:
        weights = projection[...].astype(F32)
    else:
        start = pl.multiple_of((grp_pos * groups + scalars[0]) * rows, 16)
        weights = projection[pl.ds(start, rows), :].astype(F32)
    spread = jnp.zeros((rows, LANES), F32)
    lane = lax.broadcasted_iota(jnp.int32, (rows, LANES), 1)
    for item in range(batch):
        column = jnp.sum(weights * latent_grad[item : item + 1, :], axis=1, keepdims=True)
        spread = jnp.where(lane == item, column, spread)
    for turn in range(groups):
        lines = [arrived[(branch * share + item) * groups + turn, 1:2, :] for item in range(batch)]
        if batch % 8:
            lines.append(jnp.zeros((8 - batch % 8, LANES), F32))
        sums = jnp.concatenate(lines, axis=0).T
        value = sums[:, 0:1] * latent_grad[0:1, :]
        for item in range(1, batch):
            value = value + sums[:, item : item + 1] * latent_grad[item : item + 1, :]
        grad[turn * rows : (turn + 1) * rows, :] = value[:rows]
    result = None
    for turn in range(share):
        column = jnp.sum(jnp.where(lane == (grp_pos ^ turn), spread, 0.0), axis=1, keepdims=True)
        piece = pieces[turn][: 4 * rows, :].astype(F32)
        piece = jnp.concatenate([piece[at : at + rows] for at in range(0, 4 * rows, rows)], axis=1)
        extra = arrived[(branch * share + (grp_pos ^ turn)) * groups + scalars[0]]
        means = jnp.concatenate([extra, extra], axis=0).T[:rows, 2:3]
        sums = jnp.concatenate([extra[3:4]] * (out.shape[1] // LANES), axis=1)
        term = column * (piece + means * sums)
        result = term if result is None else result + term
    out[...] = result


def assemble(slots, groups, low_count, seq_pos, branch):
    order = jnp.arange(groups, dtype=jnp.int32) ^ seq_pos
    held = jnp.stack(slots).reshape(2, groups, low_count // 2, 2, -1, LANES)[:, order]
    held = jnp.where(branch == 0, held, held[::-1])
    held = jnp.transpose(held, (2, 3, 0, 1, 4, 5)).reshape(low_count // 2, 2, 8, 8, LANES)
    return jnp.transpose(held, (0, 2, 1, 3, 4)).reshape(-1, LANES)


def body(series, time_blocks, freq_blocks, positives, conv_weight, proj_weight):
    groups = lax.axis_size("seq")
    share = lax.axis_size("grp")
    sides = lax.axis_size("pair")
    seq_pos = lax.axis_index("seq")
    branch = lax.axis_index("pair")
    grp_pos = lax.axis_index("grp")
    samples, length, own_chan = series.shape
    assert samples == 1 and sides == 2 and 4 * own_chan == LANES
    full_len = length * groups
    hidden, width = conv_weight.shape[1:]
    emb_dim = proj_weight.shape[2]
    chans = own_chan // groups
    low_count = full_len // LANES
    lows = low_count // 2
    rows = hidden // (share * groups)
    listed = time_blocks.shape[1]
    ready = chans != 8 or rows % 16 != 0
    places = jnp.stack([seq_pos, branch, grp_pos]).astype(jnp.int32)
    scalars = jnp.concatenate([places, time_blocks[0], freq_blocks[0], positives])
    weight, heads = conv_weight[0], proj_weight[0]
    picked, own_heads, mid_heads = weight, heads, heads
    if ready:
        picked = lax.dynamic_index_in_dim(weight.reshape(share, groups, rows, width), seq_pos, 1, keepdims=False)
        picked = picked.reshape(share * rows, width)
        mid_heads = lax.dynamic_index_in_dim(heads.reshape(share, groups, rows, emb_dim), seq_pos, 1, keepdims=False)
        mid_heads = mid_heads.reshape(share * rows, emb_dim)
        own_heads = lax.dynamic_slice_in_dim(heads, (grp_pos * groups + seq_pos) * rows, rows, 0)

    piece = jax.ShapeDtypeStruct((chans, length), F32)
    with jax.named_scope("arrange"):
        pieces = call(
            arrange_kernel,
            [piece] * groups,
            [HBM],
            [pltpu.SemaphoreType.DMA((groups,))],
            moved=5 * 10**5,
        )(series[0].T.reshape(groups, chans, length))
    pieces = [pieces[0]] + [
        lax.ppermute(pieces[turn], "seq", [(i, i ^ turn) for i in range(groups)]) for turn in range(1, groups)
    ]
    table = jnp.asarray(fourier_tables(full_len))
    with jax.named_scope("tables"):
        stage_one, turns, stage_two = call(
            functools.partial(tables_kernel, low_count),
            [
                jax.ShapeDtypeStruct((2 * low_count, 3 * low_count), BF16),
                jax.ShapeDtypeStruct((low_count, 2 * LANES), F32),
                jax.ShapeDtypeStruct((6 * LANES, 2 * LANES), BF16),
            ],
            [VMEM],
            flops=10**6,
            moved=10**6,
        )(table)
    with jax.named_scope("weights"):
        kernel = functools.partial(weights_kernel, groups, share, ready)
        if not ready:
            kernel = functools.partial(weights_whole, kernel)
        weights, part_weights = call(
            kernel,
            [jax.ShapeDtypeStruct((width, hidden), BF16), jax.ShapeDtypeStruct((width, share * rows), BF16)],
            [SMEM] + [VMEM] * (2 if ready else 1),
            flops=10**8,
            moved=3 * 10**6,
            room=24,
        )(*([scalars, weight, picked] if ready else [scalars, weight]))
    wire = jax.ShapeDtypeStruct((chans * low_count, LANES), BF16)
    longer = jax.ShapeDtypeStruct((chans * low_count + 16, LANES), BF16)
    with jax.named_scope("fourier"):
        own, pay = call(
            functools.partial(fourier_kernel, groups, full_len, length // 8, listed),
            [wire, longer],
            [SMEM] + [VMEM] * (3 + groups),
            [
                pltpu.VMEM((groups, chans, length), F32),
                pltpu.VMEM((chans * low_count, LANES), F32),
                pltpu.VMEM((chans * low_count, LANES), F32),
                pltpu.VMEM((chans * low_count, LANES), F32),
                pltpu.VMEM((chans * low_count, LANES), F32),
            ],
            flops=10**9,
            moved=2 * 10**6,
        )(scalars, stage_one, turns, stage_two, *pieces)

    slots = [None] * (2 * groups)
    for flip in (1, 0):
        for turn in range(groups - 2, -1, -2):
            block = pay if flip else own
            if flip or turn:
                pairs = [
                    (p * groups + i, (p ^ flip) * groups + (i ^ turn)) for p in range(2) for i in range(groups)
                ]
                block = lax.ppermute(block, ("pair", "seq"), pairs)
            slots[flip * groups + turn] = block
    for flip in range(2):
        for turn in range(0, groups, 2):
            slots[flip * groups + turn + 1] = lax.ppermute(
                slots[flip * groups + turn], "seq", [(i, i ^ 1) for i in range(groups)]
            )
    if ready:
        slots = [slot[: chans * low_count] for slot in slots]
        slots = [assemble(slots, groups, low_count, seq_pos, branch)]

    devices = sides * share * groups
    tiles = jax.ShapeDtypeStruct((lows + 4, LANES, LANES), BF16)
    with jax.named_scope("slope"):
        *grads, payload, flat = call(
            functools.partial(slope_kernel, groups, ready, 32, 4),
            [
                jax.ShapeDtypeStruct((4 * rows + (16 if turn >= share // 2 else 0), LANES), BF16)
                for turn in range(share)
            ]
            + [jax.ShapeDtypeStruct((devices, 4, LANES), F32), tiles],
            [SMEM] + [VMEM] * (2 + len(slots)),
            [
                pltpu.VMEM((lows + 4, LANES, LANES), BF16),
                pltpu.VMEM((width, share * rows), F32),
                pltpu.VMEM((8, share * rows), F32),
                pltpu.VMEM((8, share * rows), F32),
                pltpu.VMEM((share, rows, width), F32),
            ],
            flops=4 * full_len * share * rows * width,
            moved=4 * 10**6,
            room=20 + 8 * (low_count // LANES),
        )(scalars, part_weights, mid_heads, *slots)
    grads = [grads[0]] + [
        lax.ppermute(grads[turn], "grp", [(i, i ^ turn) for i in range(share)]) for turn in range(1, share)
    ]
    arrived = lax.all_to_all(payload, ("pair", "grp", "seq"), split_axis=0, concat_axis=0, tiled=True)
    near_len, columns = length // 2, 512
    with jax.named_scope("encode"):
        encoded = pl.pallas_call(
            functools.partial(encode_kernel, groups, 256),
            out_shape=jax.ShapeDtypeStruct((near_len, hidden), BF16),
            grid=(hidden // columns,),
            in_specs=[SMEM, VMEM, pl.BlockSpec((width, columns), lambda i: (0, i))],
            out_specs=pl.BlockSpec((near_len, columns), lambda i: (0, i)),
            scratch_shapes=[
                pltpu.VMEM(((lows + 4) * LANES, LANES), F32),
                pltpu.VMEM((near_len + 24, LANES), F32),
                pltpu.VMEM((2, near_len, width), BF16),
            ],
            compiler_params=pltpu.CompilerParams(vmem_limit_bytes=(20 + 12 * (low_count // LANES)) * 1024 * 1024),
            cost_estimate=pl.CostEstimate(
                flops=2 * length * hidden * width, bytes_accessed=4 * 10**6, transcendentals=length * hidden
            ),
        )(scalars, flat, weights)
    with jax.named_scope("loss"):
        loss, conv_share, proj_share = call(
            functools.partial(loss_kernel, groups, share, full_len, listed, ready),
            [
                jax.ShapeDtypeStruct((1, 1), F32),
                jax.ShapeDtypeStruct((rows, width), F32),
                jax.ShapeDtypeStruct((groups * rows, emb_dim), F32),
            ],
            [SMEM] + [VMEM] * (2 + share),
            flops=10**7,
            moved=10**6,
            out_specs=[SMEM, VMEM, VMEM],
        )(scalars, arrived, own_heads, *grads)
    return (encoded[None, None], loss.reshape(()), conv_share[None], proj_share[None])


def solution(mesh):
    in_specs = (
        P("grp", "seq", "pair"),
        P("grp", None),
        P("grp", None),
        P(),
        P("pair", None, None),
        P("pair", None, None),
    )
    out_specs = (
        P("pair", "grp", "seq", None),
        P(),
        P("pair", ("grp", "seq"), None),
        P("pair", "grp", None),
    )
    return jax.shard_map(body, mesh=mesh, in_specs=in_specs, out_specs=out_specs, check_vma=False)
```

```python
import functools
import math

import jax
import jax.numpy as jnp
import numpy as np
from jax import lax
from jax.experimental import pallas as pl
from jax.experimental.pallas import tpu as pltpu
from jax.sharding import PartitionSpec as P

TAU = 0.2
LOSS_SCALE = 256.0
LANES = 128
ROOT = math.sqrt(2.0 / math.pi)
CUBIC = 0.044715
F32 = jnp.float32
BF16 = jnp.bfloat16

VMEM = pl.BlockSpec(memory_space=pltpu.VMEM)
SMEM = pl.BlockSpec(memory_space=pltpu.SMEM)
HBM = pl.BlockSpec(memory_space=pltpu.HBM)


def call(kernel, out_shape, in_specs, scratch=(), flops=0, moved=0, room=16, out_specs=None):
    single = not isinstance(out_shape, (list, tuple))
    return pl.pallas_call(
        kernel,
        out_shape=out_shape,
        in_specs=in_specs,
        out_specs=out_specs or (VMEM if single else [VMEM] * len(out_shape)),
        scratch_shapes=list(scratch),
        compiler_params=pltpu.CompilerParams(vmem_limit_bytes=room * 1024 * 1024),
        cost_estimate=pl.CostEstimate(flops=flops, bytes_accessed=moved, transcendentals=0),
    )


def lane_order(low_count):
    inner = min(low_count, LANES)
    parts = LANES // inner
    lane = np.arange(LANES)
    return parts * (lane % inner) + lane // inner


def fourier_tables(full_len):
    low_count = full_len // LANES
    first = np.arange(low_count)
    rest = np.arange(LANES)
    second = lane_order(low_count)
    angle = (first[:, None] * first[None, :] % low_count) * (2.0 * np.pi / low_count)
    stage_one = np.concatenate([np.cos(angle), -np.sin(angle)], axis=0)
    turn = (first[:, None] * rest[None, :] % full_len) * (2.0 * np.pi / full_len)
    angle = (rest[:, None] * second[None, :] % LANES) * (2.0 * np.pi / LANES)
    cos, sin = np.cos(angle), np.sin(angle)
    stage_two = np.block([[cos, -sin], [sin, cos]])
    wide = np.zeros((2 * low_count, 2 * LANES))
    wide[:, :low_count] = stage_one
    turns = np.concatenate([np.cos(turn), np.sin(turn)], axis=1)
    return np.concatenate([stage_two, turns, wide], axis=0).astype(np.float32)


def arrange_kernel(series, *refs):
    *pieces, done = refs
    me = lax.axis_index("seq")
    copies = [pltpu.make_async_copy(series.at[me ^ turn], piece, done.at[turn]) for turn, piece in enumerate(pieces)]
    for copy in copies:
        copy.start()
    for copy in copies:
        copy.wait()


def high_low(values):
    high = values.astype(BF16)
    return high, (values - high.astype(F32)).astype(BF16)


def keep_lanes(scalars, first, number, low_count, block_len):
    lane = lax.broadcasted_iota(jnp.int32, (8, LANES), 1)
    inner = min(low_count, LANES)
    parts = LANES // inner
    high = parts * (lane % inner) + lane // inner
    block = high * low_count // block_len
    keep = jnp.ones((8, LANES), F32)
    for entry in range(first, first + number):
        keep = jnp.where(block == scalars[entry], 0.0, keep)
    return keep[0:1]


def fourier_kernel(
    groups, full_len, block_len, listed, scalars, stage_one, turns, stage_two, *refs
):
    pieces = refs[:groups]
    own, pay, gathered, steps, mags, views, wire = refs[groups:]
    me, branch = scalars[0], scalars[1]
    low_count = full_len // LANES
    chans, length = pieces[0].shape
    tops = length // LANES
    for turn in range(groups):
        gathered[turn] = pieces[turn][...]
    for source in range(groups):
        block = gathered[source ^ me]
        for top in range(tops):
            at = (source * tops + top) * chans
            steps[at : at + chans, :] = block[:, top * LANES : (top + 1) * LANES]
    columns = [steps[pl.ds(chan, low_count, stride=chans), :] for chan in range(chans)]
    high, low = high_low(jnp.concatenate(columns, axis=1))
    first = jnp.dot(stage_one[...], jnp.concatenate([high, high, low], axis=0), preferred_element_type=F32)
    cos, sin = turns[:, :LANES], turns[:, LANES:]
    turned = []
    for chan in range(chans):
        part = first[:, chan * LANES : (chan + 1) * LANES]
        part_re, part_im = part[:low_count], part[low_count:]
        turned.append(jnp.concatenate([part_re * cos + part_im * sin, part_im * cos - part_re * sin], axis=1))
    high, low = high_low(jnp.concatenate(turned, axis=0))
    second = jnp.dot(jnp.concatenate([high, high, low], axis=1), stage_two[...], preferred_element_type=F32)
    spec_re, spec_im = second[:, :LANES], second[:, LANES:]
    magnitude = jnp.sqrt(1.0 + (spec_re * spec_re + spec_im * spec_im) * (1.0 / full_len))
    mags[...] = magnitude.astype(BF16).astype(F32) * keep_lanes(scalars, 3 + listed, listed, low_count, block_len)
    time_keep = keep_lanes(scalars, 3, listed, low_count, block_len)
    for chan in range(chans):
        if low_count < LANES:
            turned_steps = columns[chan].T
            view = jnp.concatenate(
                [turned_steps[part * low_count : (part + 1) * low_count] for part in range(LANES // low_count)], axis=1
            )
        else:
            parts = low_count // LANES
            view = jnp.concatenate(
                [steps[pl.ds(chan + chans * part, LANES, stride=chans * parts), :].T for part in range(parts)], axis=0
            )
        views[chan * low_count : (chan + 1) * low_count, :] = view * time_keep

    def spread(held, out):
        for low in range(low_count):
            wire[chans * low : chans * (low + 1), :] = held[pl.ds(low, chans, stride=low_count), :]
        out[: wire.shape[0], :] = wire[...].astype(BF16)
        if out.shape[0] > wire.shape[0]:
            out[wire.shape[0] :, :] = jnp.zeros((out.shape[0] - wire.shape[0], LANES), BF16)

    @pl.when(branch == 0)
    def _():
        spread(views, own)
        spread(mags, pay)

    @pl.when(branch != 0)
    def _():
        spread(mags, own)
        spread(views, pay)


def gelu_parts(half):
    square = half * half
    return square, 1.0 + jnp.tanh(half * (2.0 * ROOT + (8.0 * ROOT * CUBIC) * square))


def stack_rows(window, count):
    return jnp.concatenate([window[6 + shift : 6 + shift + count] for shift in range(4)], axis=1).astype(BF16)


def shift_high(tile, low_count, step):
    inner = min(low_count, LANES)
    lane = lax.broadcasted_iota(jnp.int32, tile.shape, 1)
    if step < 0:
        moved = jnp.where(lane < inner, pltpu.roll(tile, (inner + 1) % LANES, 1), pltpu.roll(tile, inner % LANES, 1))
        return jnp.where(lane == 0, 0.0, moved)
    back = LANES - inner
    moved = jnp.where(lane < back, pltpu.roll(tile, back, 1), pltpu.roll(tile, (back - 1) % LANES, 1))
    return jnp.where(lane == LANES - 1, 0.0, moved)


def swap_units(values, outer, inner):
    unit = outer * inner * 8
    blocks = []
    for start in range(0, values.shape[0], unit):
        for second in range(inner):
            for first in range(outer):
                at = start + (first * inner + second) * 8
                blocks.append(values[at : at + 8])
    return jnp.concatenate(blocks, axis=0)


def tables_kernel(low_count, table, stage_one, turns, stage_two):
    high, low = high_low(table[: 2 * LANES])
    stage_two[...] = jnp.concatenate([high, low, high], axis=0)
    turns[...] = table[2 * LANES : 2 * LANES + low_count]
    high, low = high_low(table[2 * LANES + low_count :, :low_count])
    stage_one[...] = jnp.concatenate([high, low, high], axis=1)


def slope_kernel(groups, ready, merged, small, scalars, weight, projection, *refs):
    count = 1 if ready else 2 * groups
    slots = refs[:count]
    grads = refs[count:-8]
    payload, flat, odd, weights, total, pool, sample, split = refs[-8:]
    me, branch, grp_pos = scalars[0], scalars[1], scalars[2]
    lows = flat.shape[0] - 4
    low_count = 2 * lows
    share = len(grads)
    wide = 4 * LANES
    rows = total.shape[1] // share
    if ready:
        flat[2 : 2 + lows] = slots[0][...].reshape(lows, LANES, LANES)
        heads = projection[...]
        picked = weight[...]
    else:
        for flip in range(2):
            for turn in range(groups):
                at = pl.multiple_of(((branch ^ flip) * groups + (me ^ turn)) * 16, 16)
                flat[2 : 2 + lows, pl.ds(at, 16), :] = slots[flip * groups + turn][: lows * 16, :].reshape(lows, 16, LANES)
        starts = [pl.multiple_of((group * groups + me) * rows, 16) for group in range(share)]
        heads = jnp.concatenate([projection[pl.ds(start, rows), :] for start in starts], axis=0)
        picked = jnp.concatenate([weight[pl.ds(start, rows), :] for start in starts], axis=0)
    weights[...] = swap_units(0.5 * picked.astype(F32).T, 2, 8).astype(BF16)
    for edge in range(2):
        flat[edge] = shift_high(flat[lows + edge].astype(F32), low_count, -1).astype(BF16)
        flat[lows + 2 + edge] = shift_high(flat[2 + edge].astype(F32), low_count, 1).astype(BF16)
    current = flat[0].astype(F32).reshape(8, 2, 8, LANES)
    for index in range(lows + 3):
        following = flat[index + 1].astype(F32).reshape(8, 2, 8, LANES)
        mixed = jnp.concatenate([current[:, 1:2], following[:, 0:1]], axis=1)
        odd[index] = mixed.reshape(LANES, LANES).astype(BF16)
        current = following
    total[...] = jnp.zeros_like(total)
    pool[...] = jnp.zeros_like(pool)
    sample[...] = jnp.zeros_like(sample)

    def step(index, _):
        first = index * merged
        sums = pool[...]
        for source in (flat, odd):
            patches, slopes = [], []
            for item in range(0, merged, small):
                stacks = [
                    jnp.concatenate([source[first + item + at + move] for move in range(4)], axis=0)
                    for at in range(small)
                ]
                across = jnp.concatenate(stacks, axis=1)
                half = lax.dot_general(across, weights[...], (((0,), (0,)), ((), ())), preferred_element_type=F32)
                square, curve = gelu_parts(half)
                active = half * curve
                sums = sums + jnp.sum(active.reshape(small * LANES // 8, 8, active.shape[1]), axis=0)
                inner = half * (2.0 - curve) * (ROOT + (12.0 * ROOT * CUBIC) * square)
                slopes.append((curve * (0.5 + inner)).astype(BF16))
                patches.append(across)
            total[...] += jnp.dot(
                jnp.concatenate(patches, axis=1), jnp.concatenate(slopes, axis=0), preferred_element_type=F32
            )
            sample[...] += jnp.sum(slopes[0].astype(F32).reshape(small * LANES // 8, 8, -1), axis=0)
        pool[...] = sums
        return 0

    if lows == merged:
        step(0, 0)
    else:
        lax.fori_loop(0, lows // merged, step, 0)
    line = jnp.sum(pool[...], axis=0, keepdims=True)
    column = jnp.broadcast_to(line, (LANES, line.shape[1])).T
    latent = jnp.sum(column * heads.astype(F32), axis=0, keepdims=True)
    features = jnp.sum(flat[2 : 2 + lows].astype(F32), axis=0)
    features = jnp.sum(features, axis=1, keepdims=True).reshape(8, 2, 8, 1)
    features = (features[:, 0] + features[:, 1]).astype(BF16).astype(F32)
    column = jnp.broadcast_to(features[:, None], (8, 2, 8, 1)).reshape(LANES, 1)
    column = jnp.concatenate([column] * 4, axis=0)
    means = jnp.sum(sample[...], axis=0, keepdims=True) * (merged / (2.0 * small * LANES * lows))
    means = means.astype(BF16).astype(F32)
    split[...] = swap_units(total[...] - column * means, 8, 2).T.reshape(share, rows, wide)
    sums = jnp.broadcast_to(features.reshape(LANES // 2, 1), (LANES // 2, LANES)).T[0:1]
    fill = jnp.zeros((1, LANES - rows), F32)
    for target in range(share):
        part = slice(target * rows, (target + 1) * rows)
        lines = [
            latent,
            jnp.concatenate([line[:, part], fill], axis=1),
            jnp.concatenate([means[:, part], fill], axis=1),
            jnp.concatenate([sums, sums], axis=1),
        ]
        block = jnp.concatenate(lines, axis=0)
        for device in range(payload.shape[0]):
            if device // groups % share == target:
                payload[device] = block
    for turn, grad in enumerate(grads):
        part = split[grp_pos ^ turn]
        lines = [part[:, at : at + LANES] for at in range(0, wide, LANES)]
        if grad.shape[0] > 4 * rows:
            lines.append(jnp.zeros((grad.shape[0] - 4 * rows, LANES), F32))
        grad[...] = jnp.concatenate(lines, axis=0).astype(BF16)


def odd_rows(even, following):
    lane = lax.broadcasted_iota(jnp.int32, even.shape, 1)
    return jnp.where(lane < LANES // 2, pltpu.roll(even, LANES // 2, 1), pltpu.roll(following, LANES // 2, 1))


def encode_kernel(groups, chunk, columns, scalars, flat, weight, out, tall, near, patches, held, done):
    me = scalars[0]
    count, hidden = held.shape
    lows = flat.shape[0] - 4
    for index in range(lows + 4):
        tall[index * LANES : (index + 1) * LANES, :] = 0.5 * swap_units(flat[index].astype(F32), 8, 2).T
    inner = min(2 * lows, LANES)
    parts = LANES // inner
    highs = LANES // groups
    end = 8 + highs * lows
    near[0:8, :] = jnp.zeros((8, LANES), F32)
    near[end:, :] = jnp.zeros((16, LANES), F32)

    def fill(item):
        high = me * highs + item
        lane = (high % parts) * inner + high // parts
        if item == 0:
            near[6:8, :] = tall[pl.ds(lane, 2, stride=LANES), :]
        near[8 + item * lows : 8 + (item + 1) * lows, :] = tall[pl.ds(2 * LANES + lane, lows, stride=LANES), :]
        if item == highs - 1:
            near[end : end + 2, :] = tall[pl.ds((lows + 2) * LANES + lane, 2, stride=LANES), :]

    filled = 0
    copies = []
    for start in range(0, count, chunk):
        while filled < highs and filled * lows < start + chunk + 16:
            fill(filled)
            filled += 1
        for at in range(start, start + chunk, LANES):
            window = near[at : at + LANES + 24, :]
            even = window[: LANES + 16]
            patches[0, at : at + LANES, :] = stack_rows(even, LANES)
            patches[1, at : at + LANES, :] = stack_rows(odd_rows(even, window[1 : LANES + 17]), LANES)
        for column in range(0, hidden, columns):
            sums = None
            for parity in range(2):
                half = lax.dot_general(
                    patches[parity, start : start + chunk],
                    weight[column : column + columns],
                    (((1,), (1,)), ((), ())),
                    preferred_element_type=F32,
                )
                active = half * gelu_parts(half)[1]
                sums = active if sums is None else sums + active
            block = (pl.ds(start, chunk), pl.ds(column, columns))
            held[start : start + chunk, column : column + columns] = (sums * 0.5).astype(BF16)
            copies.append(pltpu.make_async_copy(held.at[block], out.at[block], done.at[len(copies)]))
            copies[-1].start()
    for copy in copies:
        copy.wait()


def loss_kernel(groups, share, full_len, listed, ready, scalars, arrived, projection, *refs):
    pieces, (loss, out, grad) = refs[:share], refs[share:]
    branch, grp_pos = scalars[1], scalars[2]
    batch = share
    latents = []
    for side in range(2):
        lines = []
        for item in range(batch):
            base = (side * share + item) * groups
            lines.append(jnp.sum(arrived[base : base + groups, 0:1, :], axis=0) * (1.0 / full_len))
        latents.append(jnp.concatenate(lines, axis=0))
    scale = [lax.rsqrt(jnp.sum(latent * latent, axis=1, keepdims=True) + 1e-06) for latent in latents]
    embs = [latent * factor for latent, factor in zip(latents, scale)]
    row = lax.broadcasted_iota(jnp.int32, (batch, LANES), 0)
    lane = lax.broadcasted_iota(jnp.int32, (batch, LANES), 1)
    logits = jnp.zeros((batch, LANES), F32)
    target = jnp.zeros((batch, LANES), F32)
    for item in range(batch):
        column = jnp.sum(embs[0] * embs[1][item : item + 1], axis=1, keepdims=True) / TAU
        logits = jnp.where(lane == item, column, logits)
        target = jnp.where((row == item) & (lane == scalars[3 + 2 * listed + item]), 1.0, target)
    inside = lane < batch
    power = jnp.where(inside, jnp.exp(logits), 0.0)
    row_sum = jnp.sum(power, axis=1, keepdims=True)
    col_sum = jnp.where(inside[0:1], jnp.sum(power, axis=0, keepdims=True), 1.0)
    value = jnp.log(col_sum) + jnp.sum(
        jnp.where(lane == 0, jnp.log(row_sum), 0.0) - 2.0 * target * logits, axis=0, keepdims=True
    )
    loss[0, 0] = jnp.sum(value) / (2.0 * batch)
    slope = (power / row_sum + power / col_sum - 2.0 * target) * (LOSS_SCALE / (2.0 * batch * TAU))
    emb_grads = [jnp.zeros((batch, LANES), F32), []]
    for item in range(batch):
        column = slope[:, item : item + 1]
        emb_grads[0] = emb_grads[0] + column * embs[1][item : item + 1]
        emb_grads[1].append(jnp.sum(column * embs[0], axis=0, keepdims=True))
    emb_grads[1] = jnp.concatenate(emb_grads[1], axis=0)
    own = []
    for side in range(2):
        inner = jnp.sum(emb_grads[side] * embs[side], axis=1, keepdims=True)
        own.append(scale[side] * (emb_grads[side] - embs[side] * inner))
    latent_grad = jnp.where(branch == 0, own[0], own[1]) * (1.0 / full_len)
    rows = out.shape[0]
    if ready:
        weights = projection[...].astype(F32)
    else:
        start = pl.multiple_of((grp_pos * groups + scalars[0]) * rows, 16)
        weights = projection[pl.ds(start, rows), :].astype(F32)
    spread = jnp.zeros((rows, LANES), F32)
    lane = lax.broadcasted_iota(jnp.int32, (rows, LANES), 1)
    for item in range(batch):
        column = jnp.sum(weights * latent_grad[item : item + 1, :], axis=1, keepdims=True)
        spread = jnp.where(lane == item, column, spread)
    for turn in range(groups):
        lines = [arrived[(branch * share + item) * groups + turn, 1:2, :] for item in range(batch)]
        if batch % 8:
            lines.append(jnp.zeros((8 - batch % 8, LANES), F32))
        sums = jnp.concatenate(lines, axis=0).T
        value = sums[:, 0:1] * latent_grad[0:1, :]
        for item in range(1, batch):
            value = value + sums[:, item : item + 1] * latent_grad[item : item + 1, :]
        grad[turn * rows : (turn + 1) * rows, :] = value[:rows]
    result = None
    for turn in range(share):
        column = jnp.sum(jnp.where(lane == (grp_pos ^ turn), spread, 0.0), axis=1, keepdims=True)
        piece = pieces[turn][: 4 * rows, :].astype(F32)
        piece = jnp.concatenate([piece[at : at + rows] for at in range(0, 4 * rows, rows)], axis=1)
        extra = arrived[(branch * share + (grp_pos ^ turn)) * groups + scalars[0]]
        means = jnp.concatenate([extra, extra], axis=0).T[:rows, 2:3]
        sums = jnp.concatenate([extra[3:4]] * (out.shape[1] // LANES), axis=1)
        term = column * (piece + means * sums)
        result = term if result is None else result + term
    out[...] = result


def assemble(slots, groups, low_count, seq_pos, branch):
    order = jnp.arange(groups, dtype=jnp.int32) ^ seq_pos
    held = jnp.stack(slots).reshape(2, groups, low_count // 2, 2, -1, LANES)[:, order]
    held = jnp.where(branch == 0, held, held[::-1])
    held = jnp.transpose(held, (2, 3, 0, 1, 4, 5)).reshape(low_count // 2, 2, 8, 8, LANES)
    return jnp.transpose(held, (0, 2, 1, 3, 4)).reshape(-1, LANES)


def body(series, time_blocks, freq_blocks, positives, conv_weight, proj_weight):
    groups = lax.axis_size("seq")
    share = lax.axis_size("grp")
    sides = lax.axis_size("pair")
    seq_pos = lax.axis_index("seq")
    branch = lax.axis_index("pair")
    grp_pos = lax.axis_index("grp")
    samples, length, own_chan = series.shape
    assert samples == 1 and sides == 2 and 4 * own_chan == LANES
    full_len = length * groups
    hidden, width = conv_weight.shape[1:]
    emb_dim = proj_weight.shape[2]
    chans = own_chan // groups
    low_count = full_len // LANES
    lows = low_count // 2
    rows = hidden // (share * groups)
    listed = time_blocks.shape[1]
    ready = chans != 8 or rows % 16 != 0
    places = jnp.stack([seq_pos, branch, grp_pos]).astype(jnp.int32)
    scalars = jnp.concatenate([places, time_blocks[0], freq_blocks[0], positives])
    weight, heads = conv_weight[0], proj_weight[0]
    picked, own_heads, mid_heads = weight, heads, heads
    if ready:
        picked = lax.dynamic_index_in_dim(weight.reshape(share, groups, rows, width), seq_pos, 1, keepdims=False)
        picked = picked.reshape(share * rows, width)
        mid_heads = lax.dynamic_index_in_dim(heads.reshape(share, groups, rows, emb_dim), seq_pos, 1, keepdims=False)
        mid_heads = mid_heads.reshape(share * rows, emb_dim)
        own_heads = lax.dynamic_slice_in_dim(heads, (grp_pos * groups + seq_pos) * rows, rows, 0)

    piece = jax.ShapeDtypeStruct((chans, length), F32)
    with jax.named_scope("arrange"):
        pieces = call(
            arrange_kernel,
            [piece] * groups,
            [HBM],
            [pltpu.SemaphoreType.DMA((groups,))],
            moved=5 * 10**5,
        )(series[0].T.reshape(groups, chans, length))
    pieces = [pieces[0]] + [
        lax.ppermute(pieces[turn], "seq", [(i, i ^ turn) for i in range(groups)]) for turn in range(1, groups)
    ]
    table = jnp.asarray(fourier_tables(full_len))
    with jax.named_scope("tables"):
        stage_one, turns, stage_two = call(
            functools.partial(tables_kernel, low_count),
            [
                jax.ShapeDtypeStruct((2 * low_count, 3 * low_count), BF16),
                jax.ShapeDtypeStruct((low_count, 2 * LANES), F32),
                jax.ShapeDtypeStruct((6 * LANES, 2 * LANES), BF16),
            ],
            [VMEM],
            flops=10**6,
            moved=10**6,
        )(table)
    wire = jax.ShapeDtypeStruct((chans * low_count, LANES), BF16)
    longer = jax.ShapeDtypeStruct((chans * low_count + 16, LANES), BF16)
    with jax.named_scope("fourier"):
        own, pay = call(
            functools.partial(fourier_kernel, groups, full_len, length // 8, listed),
            [wire, longer],
            [SMEM] + [VMEM] * (3 + groups),
            [
                pltpu.VMEM((groups, chans, length), F32),
                pltpu.VMEM((chans * low_count, LANES), F32),
                pltpu.VMEM((chans * low_count, LANES), F32),
                pltpu.VMEM((chans * low_count, LANES), F32),
                pltpu.VMEM((chans * low_count, LANES), F32),
            ],
            flops=10**9,
            moved=2 * 10**6,
        )(scalars, stage_one, turns, stage_two, *pieces)

    slots = [None] * (2 * groups)
    for flip in (1, 0):
        for turn in range(groups - 2, -1, -2):
            block = pay if flip else own
            if flip or turn:
                pairs = [
                    (p * groups + i, (p ^ flip) * groups + (i ^ turn)) for p in range(2) for i in range(groups)
                ]
                block = lax.ppermute(block, ("pair", "seq"), pairs)
            slots[flip * groups + turn] = block
    for flip in range(2):
        for turn in range(0, groups, 2):
            slots[flip * groups + turn + 1] = lax.ppermute(
                slots[flip * groups + turn], "seq", [(i, i ^ 1) for i in range(groups)]
            )
    if ready:
        slots = [slot[: chans * low_count] for slot in slots]
        slots = [assemble(slots, groups, low_count, seq_pos, branch)]

    devices = sides * share * groups
    tiles = jax.ShapeDtypeStruct((lows + 4, LANES, LANES), BF16)
    with jax.named_scope("slope"):
        *grads, payload, flat = call(
            functools.partial(slope_kernel, groups, ready, 32, 4),
            [
                jax.ShapeDtypeStruct((4 * rows + (16 if turn < share // 2 else 0), LANES), BF16)
                for turn in range(share)
            ]
            + [jax.ShapeDtypeStruct((devices, 4, LANES), F32), tiles],
            [SMEM] + [VMEM] * (2 + len(slots)),
            [
                pltpu.VMEM((lows + 4, LANES, LANES), BF16),
                pltpu.VMEM((width, share * rows), BF16),
                pltpu.VMEM((width, share * rows), F32),
                pltpu.VMEM((8, share * rows), F32),
                pltpu.VMEM((8, share * rows), F32),
                pltpu.VMEM((share, rows, width), F32),
            ],
            flops=4 * full_len * share * rows * width,
            moved=4 * 10**6,
            room=20 + 8 * (low_count // LANES),
        )(scalars, picked, mid_heads, *slots)
    grads = [grads[0]] + [
        lax.ppermute(grads[turn], "grp", [(i, i ^ turn) for i in range(share)]) for turn in range(1, share)
    ]
    arrived = lax.all_to_all(payload, ("pair", "grp", "seq"), split_axis=0, concat_axis=0, tiled=True)
    near_len, chunk, columns = length // 2, 512, 256
    with jax.named_scope("encode"):
        encoded = pl.pallas_call(
            functools.partial(encode_kernel, groups, chunk, columns),
            out_shape=jax.ShapeDtypeStruct((near_len, hidden), BF16),
            in_specs=[SMEM, VMEM, VMEM],
            out_specs=HBM,
            scratch_shapes=[
                pltpu.VMEM(((lows + 4) * LANES, LANES), F32),
                pltpu.VMEM((near_len + 24, LANES), F32),
                pltpu.VMEM((2, near_len, width), BF16),
                pltpu.VMEM((near_len, hidden), BF16),
                pltpu.SemaphoreType.DMA(((near_len // chunk) * (hidden // columns),)),
            ],
            compiler_params=pltpu.CompilerParams(vmem_limit_bytes=(24 + 12 * (low_count // LANES)) * 1024 * 1024),
            cost_estimate=pl.CostEstimate(
                flops=2 * length * hidden * width, bytes_accessed=4 * 10**6, transcendentals=length * hidden
            ),
        )(scalars, flat, weight)
    with jax.named_scope("loss"):
        loss, conv_share, proj_share = call(
            functools.partial(loss_kernel, groups, share, full_len, listed, ready),
            [
                jax.ShapeDtypeStruct((1, 1), F32),
                jax.ShapeDtypeStruct((rows, width), F32),
                jax.ShapeDtypeStruct((groups * rows, emb_dim), F32),
            ],
            [SMEM] + [VMEM] * (2 + share),
            flops=10**7,
            moved=10**6,
            out_specs=[SMEM, VMEM, VMEM],
        )(scalars, arrived, own_heads, *grads)
    return (encoded[None, None], loss.reshape(()), conv_share[None], proj_share[None])


def solution(mesh):
    in_specs = (
        P("grp", "seq", "pair"),
        P("grp", None),
        P("grp", None),
        P(),
        P("pair", None, None),
        P("pair", None, None),
    )
    out_specs = (
        P("pair", "grp", "seq", None),
        P(),
        P("pair", ("grp", "seq"), None),
        P("pair", "grp", None),
    )
    return jax.shard_map(body, mesh=mesh, in_specs=in_specs, out_specs=out_specs, check_vma=False)
```

```python
import functools
import math

import jax
import jax.numpy as jnp
import numpy as np
from jax import lax
from jax.experimental import pallas as pl
from jax.experimental.pallas import tpu as pltpu
from jax.sharding import PartitionSpec as P

TAU = 0.2
LOSS_SCALE = 256.0
LANES = 128
ROOT = math.sqrt(2.0 / math.pi)
CUBIC = 0.044715
F32 = jnp.float32
BF16 = jnp.bfloat16

VMEM = pl.BlockSpec(memory_space=pltpu.VMEM)
SMEM = pl.BlockSpec(memory_space=pltpu.SMEM)
HBM = pl.BlockSpec(memory_space=pltpu.HBM)


def call(kernel, out_shape, in_specs, scratch=(), flops=0, moved=0, room=16, out_specs=None):
    single = not isinstance(out_shape, (list, tuple))
    return pl.pallas_call(
        kernel,
        out_shape=out_shape,
        in_specs=in_specs,
        out_specs=out_specs or (VMEM if single else [VMEM] * len(out_shape)),
        scratch_shapes=list(scratch),
        compiler_params=pltpu.CompilerParams(vmem_limit_bytes=room * 1024 * 1024),
        cost_estimate=pl.CostEstimate(flops=flops, bytes_accessed=moved, transcendentals=0),
    )


def lane_order(low_count):
    inner = min(low_count, LANES)
    parts = LANES // inner
    lane = np.arange(LANES)
    return parts * (lane % inner) + lane // inner


def fourier_tables(full_len):
    low_count = full_len // LANES
    first = np.arange(low_count)
    rest = np.arange(LANES)
    second = lane_order(low_count)
    angle = (first[:, None] * first[None, :] % low_count) * (2.0 * np.pi / low_count)
    stage_one = np.concatenate([np.cos(angle), -np.sin(angle)], axis=0)
    turn = (first[:, None] * rest[None, :] % full_len) * (2.0 * np.pi / full_len)
    angle = (rest[:, None] * second[None, :] % LANES) * (2.0 * np.pi / LANES)
    cos, sin = np.cos(angle), np.sin(angle)
    stage_two = np.block([[cos, -sin], [sin, cos]])
    wide = np.zeros((2 * low_count, 2 * LANES))
    wide[:, :low_count] = stage_one
    turns = np.concatenate([np.cos(turn), np.sin(turn)], axis=1)
    return np.concatenate([stage_two, turns, wide], axis=0).astype(np.float32)


def arrange_kernel(series, *refs):
    *pieces, done = refs
    me = lax.axis_index("seq")
    copies = [pltpu.make_async_copy(series.at[me ^ turn], piece, done.at[turn]) for turn, piece in enumerate(pieces)]
    for copy in copies:
        copy.start()
    for copy in copies:
        copy.wait()


def high_low(values):
    high = values.astype(BF16)
    return high, (values - high.astype(F32)).astype(BF16)


def keep_lanes(scalars, first, number, low_count, block_len):
    lane = lax.broadcasted_iota(jnp.int32, (8, LANES), 1)
    inner = min(low_count, LANES)
    parts = LANES // inner
    high = parts * (lane % inner) + lane // inner
    block = high * low_count // block_len
    keep = jnp.ones((8, LANES), F32)
    for entry in range(first, first + number):
        keep = jnp.where(block == scalars[entry], 0.0, keep)
    return keep[0:1]


def fourier_kernel(
    groups, full_len, block_len, listed, scalars, stage_one, turns, stage_two, *refs
):
    pieces = refs[:groups]
    own, pay, gathered, steps, mags, views, wire = refs[groups:]
    me, branch = scalars[0], scalars[1]
    low_count = full_len // LANES
    chans, length = pieces[0].shape
    tops = length // LANES
    for turn in range(groups):
        gathered[turn] = pieces[turn][...]
    for source in range(groups):
        block = gathered[source ^ me]
        for top in range(tops):
            at = (source * tops + top) * chans
            steps[at : at + chans, :] = block[:, top * LANES : (top + 1) * LANES]
    columns = [steps[pl.ds(chan, low_count, stride=chans), :] for chan in range(chans)]
    high, low = high_low(jnp.concatenate(columns, axis=1))
    first = jnp.dot(stage_one[...], jnp.concatenate([high, high, low], axis=0), preferred_element_type=F32)
    cos, sin = turns[:, :LANES], turns[:, LANES:]
    turned = []
    for chan in range(chans):
        part = first[:, chan * LANES : (chan + 1) * LANES]
        part_re, part_im = part[:low_count], part[low_count:]
        turned.append(jnp.concatenate([part_re * cos + part_im * sin, part_im * cos - part_re * sin], axis=1))
    high, low = high_low(jnp.concatenate(turned, axis=0))
    second = jnp.dot(jnp.concatenate([high, high, low], axis=1), stage_two[...], preferred_element_type=F32)
    spec_re, spec_im = second[:, :LANES], second[:, LANES:]
    magnitude = jnp.sqrt(1.0 + (spec_re * spec_re + spec_im * spec_im) * (1.0 / full_len))
    mags[...] = magnitude.astype(BF16).astype(F32) * keep_lanes(scalars, 3 + listed, listed, low_count, block_len)
    time_keep = keep_lanes(scalars, 3, listed, low_count, block_len)
    for chan in range(chans):
        if low_count < LANES:
            turned_steps = columns[chan].T
            view = jnp.concatenate(
                [turned_steps[part * low_count : (part + 1) * low_count] for part in range(LANES // low_count)], axis=1
            )
        else:
            parts = low_count // LANES
            view = jnp.concatenate(
                [steps[pl.ds(chan + chans * part, LANES, stride=chans * parts), :].T for part in range(parts)], axis=0
            )
        views[chan * low_count : (chan + 1) * low_count, :] = view * time_keep

    def spread(held, out):
        for low in range(low_count):
            wire[chans * low : chans * (low + 1), :] = held[pl.ds(low, chans, stride=low_count), :]
        out[: wire.shape[0], :] = wire[...].astype(BF16)
        if out.shape[0] > wire.shape[0]:
            out[wire.shape[0] :, :] = jnp.zeros((out.shape[0] - wire.shape[0], LANES), BF16)

    @pl.when(branch == 0)
    def _():
        spread(views, own)
        spread(mags, pay)

    @pl.when(branch != 0)
    def _():
        spread(mags, own)
        spread(views, pay)


def gelu_parts(half):
    square = half * half
    return square, 1.0 + jnp.tanh(half * (2.0 * ROOT + (8.0 * ROOT * CUBIC) * square))


def stack_rows(window, count):
    return jnp.concatenate([window[6 + shift : 6 + shift + count] for shift in range(4)], axis=1).astype(BF16)


def shift_high(tile, low_count, step):
    inner = min(low_count, LANES)
    lane = lax.broadcasted_iota(jnp.int32, tile.shape, 1)
    if step < 0:
        moved = jnp.where(lane < inner, pltpu.roll(tile, (inner + 1) % LANES, 1), pltpu.roll(tile, inner % LANES, 1))
        return jnp.where(lane == 0, 0.0, moved)
    back = LANES - inner
    moved = jnp.where(lane < back, pltpu.roll(tile, back, 1), pltpu.roll(tile, (back - 1) % LANES, 1))
    return jnp.where(lane == LANES - 1, 0.0, moved)


def swap_units(values, outer, inner):
    unit = outer * inner * 8
    blocks = []
    for start in range(0, values.shape[0], unit):
        for second in range(inner):
            for first in range(outer):
                at = start + (first * inner + second) * 8
                blocks.append(values[at : at + 8])
    return jnp.concatenate(blocks, axis=0)


def tables_kernel(low_count, table, stage_one, turns, stage_two):
    high, low = high_low(table[: 2 * LANES])
    stage_two[...] = jnp.concatenate([high, low, high], axis=0)
    turns[...] = table[2 * LANES : 2 * LANES + low_count]
    high, low = high_low(table[2 * LANES + low_count :, :low_count])
    stage_one[...] = jnp.concatenate([high, low, high], axis=1)


def slope_kernel(groups, ready, merged, small, scalars, weight, projection, *refs):
    count = 1 if ready else 2 * groups
    slots = refs[:count]
    grads = refs[count:-8]
    payload, flat, odd, weights, total, pool, sample, split = refs[-8:]
    me, branch, grp_pos = scalars[0], scalars[1], scalars[2]
    lows = flat.shape[0] - 4
    low_count = 2 * lows
    share = len(grads)
    wide = 4 * LANES
    rows = total.shape[1] // share
    if ready:
        flat[2 : 2 + lows] = slots[0][...].reshape(lows, LANES, LANES)
        heads = projection[...]
        picked = weight[...]
    else:
        for flip in range(2):
            for turn in range(groups):
                at = pl.multiple_of(((branch ^ flip) * groups + (me ^ turn)) * 16, 16)
                flat[2 : 2 + lows, pl.ds(at, 16), :] = slots[flip * groups + turn][: lows * 16, :].reshape(lows, 16, LANES)
        starts = [pl.multiple_of((group * groups + me) * rows, 16) for group in range(share)]
        heads = jnp.concatenate([projection[pl.ds(start, rows), :] for start in starts], axis=0)
        picked = jnp.concatenate([weight[pl.ds(start, rows), :] for start in starts], axis=0)
    weights[...] = swap_units(0.5 * picked.astype(F32).T, 2, 8).astype(BF16)
    for edge in range(2):
        flat[edge] = shift_high(flat[lows + edge].astype(F32), low_count, -1).astype(BF16)
        flat[lows + 2 + edge] = shift_high(flat[2 + edge].astype(F32), low_count, 1).astype(BF16)
    current = flat[0].astype(F32).reshape(8, 2, 8, LANES)
    for index in range(lows + 3):
        following = flat[index + 1].astype(F32).reshape(8, 2, 8, LANES)
        mixed = jnp.concatenate([current[:, 1:2], following[:, 0:1]], axis=1)
        odd[index] = mixed.reshape(LANES, LANES).astype(BF16)
        current = following
    total[...] = jnp.zeros_like(total)
    pool[...] = jnp.zeros_like(pool)
    sample[...] = jnp.zeros_like(sample)

    def step(index, _):
        first = index * merged
        sums = pool[...]
        for source in (flat, odd):
            patches, slopes = [], []
            for item in range(0, merged, small):
                stacks = [
                    jnp.concatenate([source[first + item + at + move] for move in range(4)], axis=0)
                    for at in range(small)
                ]
                across = jnp.concatenate(stacks, axis=1)
                half = lax.dot_general(across, weights[...], (((0,), (0,)), ((), ())), preferred_element_type=F32)
                square, curve = gelu_parts(half)
                active = half * curve
                sums = sums + jnp.sum(active.reshape(small * LANES // 8, 8, active.shape[1]), axis=0)
                inner = half * (2.0 - curve) * (ROOT + (12.0 * ROOT * CUBIC) * square)
                slopes.append((curve * (0.5 + inner)).astype(BF16))
                patches.append(across)
            total[...] += jnp.dot(
                jnp.concatenate(patches, axis=1), jnp.concatenate(slopes, axis=0), preferred_element_type=F32
            )
            sample[...] += jnp.sum(slopes[0].astype(F32).reshape(small * LANES // 8, 8, -1), axis=0)
        pool[...] = sums
        return 0

    if lows == merged:
        step(0, 0)
    else:
        lax.fori_loop(0, lows // merged, step, 0)
    line = jnp.sum(pool[...], axis=0, keepdims=True)
    column = jnp.broadcast_to(line, (LANES, line.shape[1])).T
    latent = jnp.sum(column * heads.astype(F32), axis=0, keepdims=True)
    features = jnp.sum(flat[2 : 2 + lows].astype(F32), axis=0)
    features = jnp.sum(features, axis=1, keepdims=True).reshape(8, 2, 8, 1)
    features = (features[:, 0] + features[:, 1]).astype(BF16).astype(F32)
    column = jnp.broadcast_to(features[:, None], (8, 2, 8, 1)).reshape(LANES, 1)
    column = jnp.concatenate([column] * 4, axis=0)
    means = jnp.sum(sample[...], axis=0, keepdims=True) * (merged / (2.0 * small * LANES * lows))
    means = means.astype(BF16).astype(F32)
    split[...] = swap_units(total[...] - column * means, 8, 2).T.reshape(share, rows, wide)
    sums = jnp.broadcast_to(features.reshape(LANES // 2, 1), (LANES // 2, LANES)).T[0:1]
    fill = jnp.zeros((1, LANES - rows), F32)
    for target in range(share):
        part = slice(target * rows, (target + 1) * rows)
        lines = [
            latent,
            jnp.concatenate([line[:, part], fill], axis=1),
            jnp.concatenate([means[:, part], fill], axis=1),
            jnp.concatenate([sums, sums], axis=1),
        ]
        block = jnp.concatenate(lines, axis=0)
        for device in range(payload.shape[0]):
            if device // groups % share == target:
                payload[device] = block
    for turn, grad in enumerate(grads):
        part = split[grp_pos ^ turn]
        lines = [part[:, at : at + LANES] for at in range(0, wide, LANES)]
        if grad.shape[0] > 4 * rows:
            lines.append(jnp.zeros((grad.shape[0] - 4 * rows, LANES), F32))
        grad[...] = jnp.concatenate(lines, axis=0).astype(BF16)


def odd_rows(even, following):
    lane = lax.broadcasted_iota(jnp.int32, even.shape, 1)
    return jnp.where(lane < LANES // 2, pltpu.roll(even, LANES // 2, 1), pltpu.roll(following, LANES // 2, 1))


def encode_kernel(groups, chunk, columns, scalars, flat, weight, out, tall, near, patches, held, done):
    me = scalars[0]
    count, hidden = held.shape
    lows = flat.shape[0] - 4
    for index in range(lows + 4):
        tall[index * LANES : (index + 1) * LANES, :] = 0.5 * swap_units(flat[index].astype(F32), 8, 2).T
    inner = min(2 * lows, LANES)
    parts = LANES // inner
    highs = LANES // groups
    end = 8 + highs * lows
    near[0:8, :] = jnp.zeros((8, LANES), F32)
    near[end:, :] = jnp.zeros((16, LANES), F32)

    def fill(item):
        high = me * highs + item
        lane = (high % parts) * inner + high // parts
        if item == 0:
            near[6:8, :] = tall[pl.ds(lane, 2, stride=LANES), :]
        near[8 + item * lows : 8 + (item + 1) * lows, :] = tall[pl.ds(2 * LANES + lane, lows, stride=LANES), :]
        if item == highs - 1:
            near[end : end + 2, :] = tall[pl.ds((lows + 2) * LANES + lane, 2, stride=LANES), :]

    filled = 0
    copies = []
    for start in range(0, count, chunk):
        while filled < highs and filled * lows < start + chunk + 16:
            fill(filled)
            filled += 1
        for at in range(start, start + chunk, LANES):
            window = near[at : at + LANES + 24, :]
            even = window[: LANES + 16]
            patches[0, at : at + LANES, :] = stack_rows(even, LANES)
            patches[1, at : at + LANES, :] = stack_rows(odd_rows(even, window[1 : LANES + 17]), LANES)
        for column in range(0, hidden, columns):
            sums = None
            for parity in range(2):
                half = lax.dot_general(
                    patches[parity, start : start + chunk],
                    weight[column : column + columns],
                    (((1,), (1,)), ((), ())),
                    preferred_element_type=F32,
                )
                active = half * gelu_parts(half)[1]
                sums = active if sums is None else sums + active
            block = (pl.ds(start, chunk), pl.ds(column, columns))
            held[start : start + chunk, column : column + columns] = (sums * 0.5).astype(BF16)
            copies.append(pltpu.make_async_copy(held.at[block], out.at[block], done.at[len(copies)]))
            copies[-1].start()
    for copy in copies:
        copy.wait()


def loss_kernel(groups, share, full_len, listed, ready, scalars, arrived, projection, *refs):
    pieces, (loss, out, grad) = refs[:share], refs[share:]
    branch, grp_pos = scalars[1], scalars[2]
    batch = share
    latents = []
    for side in range(2):
        lines = []
        for item in range(batch):
            base = (side * share + item) * groups
            lines.append(jnp.sum(arrived[base : base + groups, 0:1, :], axis=0) * (1.0 / full_len))
        latents.append(jnp.concatenate(lines, axis=0))
    scale = [lax.rsqrt(jnp.sum(latent * latent, axis=1, keepdims=True) + 1e-06) for latent in latents]
    embs = [latent * factor for latent, factor in zip(latents, scale)]
    row = lax.broadcasted_iota(jnp.int32, (batch, LANES), 0)
    lane = lax.broadcasted_iota(jnp.int32, (batch, LANES), 1)
    logits = jnp.zeros((batch, LANES), F32)
    target = jnp.zeros((batch, LANES), F32)
    for item in range(batch):
        column = jnp.sum(embs[0] * embs[1][item : item + 1], axis=1, keepdims=True) / TAU
        logits = jnp.where(lane == item, column, logits)
        target = jnp.where((row == item) & (lane == scalars[3 + 2 * listed + item]), 1.0, target)
    inside = lane < batch
    power = jnp.where(inside, jnp.exp(logits), 0.0)
    row_sum = jnp.sum(power, axis=1, keepdims=True)
    col_sum = jnp.where(inside[0:1], jnp.sum(power, axis=0, keepdims=True), 1.0)
    value = jnp.log(col_sum) + jnp.sum(
        jnp.where(lane == 0, jnp.log(row_sum), 0.0) - 2.0 * target * logits, axis=0, keepdims=True
    )
    loss[0, 0] = jnp.sum(value) / (2.0 * batch)
    slope = (power / row_sum + power / col_sum - 2.0 * target) * (LOSS_SCALE / (2.0 * batch * TAU))
    emb_grads = [jnp.zeros((batch, LANES), F32), []]
    for item in range(batch):
        column = slope[:, item : item + 1]
        emb_grads[0] = emb_grads[0] + column * embs[1][item : item + 1]
        emb_grads[1].append(jnp.sum(column * embs[0], axis=0, keepdims=True))
    emb_grads[1] = jnp.concatenate(emb_grads[1], axis=0)
    own = []
    for side in range(2):
        inner = jnp.sum(emb_grads[side] * embs[side], axis=1, keepdims=True)
        own.append(scale[side] * (emb_grads[side] - embs[side] * inner))
    latent_grad = jnp.where(branch == 0, own[0], own[1]) * (1.0 / full_len)
    rows = out.shape[0]
    if ready:
        weights = projection[...].astype(F32)
    else:
        start = pl.multiple_of((grp_pos * groups + scalars[0]) * rows, 16)
        weights = projection[pl.ds(start, rows), :].astype(F32)
    for turn in range(groups):
        lines = [arrived[(branch * share + item) * groups + turn, 1:2, :] for item in range(batch)]
        if batch % 8:
            lines.append(jnp.zeros((8 - batch % 8, LANES), F32))
        sums = jnp.concatenate(lines, axis=0).T
        value = sums[:, 0:1] * latent_grad[0:1, :]
        for item in range(1, batch):
            value = value + sums[:, item : item + 1] * latent_grad[item : item + 1, :]
        grad[turn * rows : (turn + 1) * rows, :] = value[:rows]
    result = None
    for turn in range(share):
        line = jnp.sum(jnp.where(row == (grp_pos ^ turn), latent_grad, 0.0), axis=0, keepdims=True)
        column = jnp.sum(weights * line, axis=1, keepdims=True)
        piece = pieces[turn][: 4 * rows, :].astype(F32)
        piece = jnp.concatenate([piece[at : at + rows] for at in range(0, 4 * rows, rows)], axis=1)
        extra = arrived[(branch * share + (grp_pos ^ turn)) * groups + scalars[0]]
        means = jnp.concatenate([extra, extra], axis=0).T[:rows, 2:3]
        sums = jnp.concatenate([extra[3:4]] * (out.shape[1] // LANES), axis=1)
        term = column * (piece + means * sums)
        result = term if result is None else result + term
    out[...] = result


def assemble(slots, groups, low_count, seq_pos, branch):
    order = jnp.arange(groups, dtype=jnp.int32) ^ seq_pos
    held = jnp.stack(slots).reshape(2, groups, low_count // 2, 2, -1, LANES)[:, order]
    held = jnp.where(branch == 0, held, held[::-1])
    held = jnp.transpose(held, (2, 3, 0, 1, 4, 5)).reshape(low_count // 2, 2, 8, 8, LANES)
    return jnp.transpose(held, (0, 2, 1, 3, 4)).reshape(-1, LANES)


def body(series, time_blocks, freq_blocks, positives, conv_weight, proj_weight):
    groups = lax.axis_size("seq")
    share = lax.axis_size("grp")
    sides = lax.axis_size("pair")
    seq_pos = lax.axis_index("seq")
    branch = lax.axis_index("pair")
    grp_pos = lax.axis_index("grp")
    samples, length, own_chan = series.shape
    assert samples == 1 and sides == 2 and 4 * own_chan == LANES
    full_len = length * groups
    hidden, width = conv_weight.shape[1:]
    emb_dim = proj_weight.shape[2]
    chans = own_chan // groups
    low_count = full_len // LANES
    lows = low_count // 2
    rows = hidden // (share * groups)
    listed = time_blocks.shape[1]
    ready = chans != 8 or rows % 16 != 0
    places = jnp.stack([seq_pos, branch, grp_pos]).astype(jnp.int32)
    scalars = jnp.concatenate([places, time_blocks[0], freq_blocks[0], positives])
    weight, heads = conv_weight[0], proj_weight[0]
    picked, own_heads, mid_heads = weight, heads, heads
    if ready:
        picked = lax.dynamic_index_in_dim(weight.reshape(share, groups, rows, width), seq_pos, 1, keepdims=False)
        picked = picked.reshape(share * rows, width)
        mid_heads = lax.dynamic_index_in_dim(heads.reshape(share, groups, rows, emb_dim), seq_pos, 1, keepdims=False)
        mid_heads = mid_heads.reshape(share * rows, emb_dim)
        own_heads = lax.dynamic_slice_in_dim(heads, (grp_pos * groups + seq_pos) * rows, rows, 0)

    piece = jax.ShapeDtypeStruct((chans, length), F32)
    with jax.named_scope("arrange"):
        pieces = call(
            arrange_kernel,
            [piece] * groups,
            [HBM],
            [pltpu.SemaphoreType.DMA((groups,))],
            moved=5 * 10**5,
        )(series[0].T.reshape(groups, chans, length))
    pieces = [pieces[0]] + [
        lax.ppermute(pieces[turn], "seq", [(i, i ^ turn) for i in range(groups)]) for turn in range(1, groups)
    ]
    table = jnp.asarray(fourier_tables(full_len))
    with jax.named_scope("tables"):
        stage_one, turns, stage_two = call(
            functools.partial(tables_kernel, low_count),
            [
                jax.ShapeDtypeStruct((2 * low_count, 3 * low_count), BF16),
                jax.ShapeDtypeStruct((low_count, 2 * LANES), F32),
                jax.ShapeDtypeStruct((6 * LANES, 2 * LANES), BF16),
            ],
            [VMEM],
            flops=10**6,
            moved=10**6,
        )(table)
    wire = jax.ShapeDtypeStruct((chans * low_count, LANES), BF16)
    longer = wire
    with jax.named_scope("fourier"):
        own, pay = call(
            functools.partial(fourier_kernel, groups, full_len, length // 8, listed),
            [wire, longer],
            [SMEM] + [VMEM] * (3 + groups),
            [
                pltpu.VMEM((groups, chans, length), F32),
                pltpu.VMEM((chans * low_count, LANES), F32),
                pltpu.VMEM((chans * low_count, LANES), F32),
                pltpu.VMEM((chans * low_count, LANES), F32),
                pltpu.VMEM((chans * low_count, LANES), F32),
            ],
            flops=10**9,
            moved=2 * 10**6,
        )(scalars, stage_one, turns, stage_two, *pieces)

    slots = [None] * (2 * groups)
    for flip in (1, 0):
        for turn in range(groups - 2, -1, -2):
            block = pay if flip else own
            if flip or turn:
                pairs = [
                    (p * groups + i, (p ^ flip) * groups + (i ^ turn)) for p in range(2) for i in range(groups)
                ]
                block = lax.ppermute(block, ("pair", "seq"), pairs)
            slots[flip * groups + turn] = block
    for flip in range(2):
        for turn in range(0, groups, 2):
            slots[flip * groups + turn + 1] = lax.ppermute(
                slots[flip * groups + turn], "seq", [(i, i ^ 1) for i in range(groups)]
            )
    if ready:
        slots = [slot[: chans * low_count] for slot in slots]
        slots = [assemble(slots, groups, low_count, seq_pos, branch)]

    devices = sides * share * groups
    tiles = jax.ShapeDtypeStruct((lows + 4, LANES, LANES), BF16)
    with jax.named_scope("slope"):
        *grads, payload, flat = call(
            functools.partial(slope_kernel, groups, ready, 32, 4),
            [
                jax.ShapeDtypeStruct((4 * rows + (16 if turn < share // 2 else 0), LANES), BF16)
                for turn in range(share)
            ]
            + [jax.ShapeDtypeStruct((devices, 4, LANES), F32), tiles],
            [SMEM] + [VMEM] * (2 + len(slots)),
            [
                pltpu.VMEM((lows + 4, LANES, LANES), BF16),
                pltpu.VMEM((width, share * rows), BF16),
                pltpu.VMEM((width, share * rows), F32),
                pltpu.VMEM((8, share * rows), F32),
                pltpu.VMEM((8, share * rows), F32),
                pltpu.VMEM((share, rows, width), F32),
            ],
            flops=4 * full_len * share * rows * width,
            moved=4 * 10**6,
            room=20 + 8 * (low_count // LANES),
        )(scalars, picked, mid_heads, *slots)
    grads = [grads[0]] + [
        lax.ppermute(grads[turn], "grp", [(i, i ^ turn) for i in range(share)]) for turn in range(1, share)
    ]
    arrived = lax.all_to_all(payload, ("pair", "grp", "seq"), split_axis=0, concat_axis=0, tiled=True)
    near_len, chunk, columns = length // 2, 512, 256
    with jax.named_scope("encode"):
        encoded = pl.pallas_call(
            functools.partial(encode_kernel, groups, chunk, columns),
            out_shape=jax.ShapeDtypeStruct((near_len, hidden), BF16),
            in_specs=[SMEM, VMEM, VMEM],
            out_specs=HBM,
            scratch_shapes=[
                pltpu.VMEM(((lows + 4) * LANES, LANES), F32),
                pltpu.VMEM((near_len + 24, LANES), F32),
                pltpu.VMEM((2, near_len, width), BF16),
                pltpu.VMEM((near_len, hidden), BF16),
                pltpu.SemaphoreType.DMA(((near_len // chunk) * (hidden // columns),)),
            ],
            compiler_params=pltpu.CompilerParams(vmem_limit_bytes=(24 + 12 * (low_count // LANES)) * 1024 * 1024),
            cost_estimate=pl.CostEstimate(
                flops=2 * length * hidden * width, bytes_accessed=4 * 10**6, transcendentals=length * hidden
            ),
        )(scalars, flat, weight)
    with jax.named_scope("loss"):
        loss, conv_share, proj_share = call(
            functools.partial(loss_kernel, groups, share, full_len, listed, ready),
            [
                jax.ShapeDtypeStruct((1, 1), F32),
                jax.ShapeDtypeStruct((rows, width), F32),
                jax.ShapeDtypeStruct((groups * rows, emb_dim), F32),
            ],
            [SMEM] + [VMEM] * (2 + share),
            flops=10**7,
            moved=10**6,
            out_specs=[SMEM, VMEM, VMEM],
        )(scalars, arrived, own_heads, *grads)
    return (encoded[None, None], loss.reshape(()), conv_share[None], proj_share[None])


def solution(mesh):
    in_specs = (
        P("grp", "seq", "pair"),
        P("grp", None),
        P("grp", None),
        P(),
        P("pair", None, None),
        P("pair", None, None),
    )
    out_specs = (
        P("pair", "grp", "seq", None),
        P(),
        P("pair", ("grp", "seq"), None),
        P("pair", "grp", None),
    )
    return jax.shard_map(body, mesh=mesh, in_specs=in_specs, out_specs=out_specs, check_vma=False)
```
